1024 devices in a mesh: dp: 64 (over y, x), mp: 16 (over z, core).
Axes of the slice: x: 8, y: 8, z: 8, core: 2. Of those that a mesh axis runs over, the one named last changes fastest.
Arguments:
- events: bfloat16 [32768, 512], P('dp'), may hold values from -6 to 6
- in_proj: bfloat16 [512, 16, 128], P(None, 'mp'), may hold values from -1 to 1
- out_proj: bfloat16 [16, 32, 512], P('mp'), may hold values from -1 to 1
- lengths: int32 [64, 8], P('dp'), may hold values from 1 to 256, 512 in all within a row
- targets: bfloat16 [32768, 512], P('dp'), may hold values from -6 to 6
- item_table: bfloat16 [262144, 512], P(('dp', 'mp')), may hold values from -6 to 6
- sample_ids: int32 [8192], P(('dp', 'mp')), may hold values from 0 to 262143, as said below
- sample_counts: int32 [8192], P(('dp', 'mp')), may hold values from 1 to 64
Outputs:
- loss: float32 [32768], P('dp')
- d_user: float32 [32768, 512], P(('dp', 'mp'))
- d_samples: float32 [8192, 512], P(('dp', 'mp'))
The draws below stay inside these ranges and needn't reach their ends.
Inputs may be any that keep to these rules, and one draw needn't show every extreme that they name: `sample_ids`: the sampled slots of device block k (slots k * 8 to (k + 1) * 8 - 1, blocks in the order of dp+mp) name rows k * 256 to (k + 1) * 256 - 1 of the table; an item may be named twice.
All inputs are finite; a program needn't handle non-finite values.
Results may differ from the reference program's by a relative error of at most 0.0036.
Values may be sent and summed in bfloat16 or wider, within the bound.
No kernel may reach another device: no remote copies, remote signals or barrier semaphores. Data moves between devices by JAX's collectives and lax.ppermute only.
A program may use at most 32 MiB of HBM per device.

```python
import math
import jax
import jax.numpy as jnp
import numpy as np
from jax import lax

D = 512
DH = 32
TOK_DEV = 512
ROWS_DEV = 256
SLOTS_DEV = 8
HEADS = 16
SEQS_DEV = 8
MAXLEN = 256
GROUPS = 64
TOKENS = 32768
NSAMP = 8192
ITEMS = 262144


def draw_sample_ids(key, part):
    key = jax.random.fold_in(key, 7)
    offsets = jax.random.randint(key, (NSAMP,), 0, ROWS_DEV, dtype=jnp.int32)
    blocks = jnp.arange(NSAMP, dtype=jnp.int32) // SLOTS_DEV
    return (blocks * ROWS_DEV + offsets).astype(jnp.int32)


def draw_in_proj(key, part):
    key = jax.random.fold_in(key, 11)
    base = jnp.clip(jax.random.normal(key, (D, HEADS, 4 * DH), jnp.float32), -6.0, 6.0) / jnp.sqrt(jnp.float32(D))
    head_pos = jnp.arange(HEADS, dtype=jnp.float32) / jnp.float32(max(HEADS - 1, 1))
    head_scale = 0.6 * jnp.power(3.0, head_pos)
    column_block = jnp.arange(4 * DH, dtype=jnp.int32) // DH
    scale = jnp.where(column_block[None, :] == 1, head_scale[:, None], 1.0)
    return (base * scale[None, :, :]).astype(jnp.bfloat16)


def place_ends(values, rng, smallest, largest):
    longest = values.shape.index(max(values.shape))
    spots = []
    for shift in (0, 1):
        where = [jax.random.randint(jax.random.fold_in(rng, axis), (), 0, length) for axis, length in enumerate(values.shape)]
        where[longest] = (where[longest] + shift) % values.shape[longest]
        spots.append(tuple(where))
    return values.at[spots[0]].set(smallest).at[spots[1]].set(largest)


def steps_of(rng, extent, shards, low, high):
    loudness, own = 1.0, jax.random.fold_in(rng, 6)
    for axis_at, blocks in shards:
        draws = jnp.exp(jax.random.uniform(jax.random.fold_in(own, axis_at), (blocks,), jnp.float32, low / len(shards), high / len(shards)))
        loudness = loudness * jnp.repeat(draws, extent[axis_at] // blocks).reshape([-1 if axis == axis_at else 1 for axis in range(len(extent))])
    return loudness


def split_up(number_of, total, most, skew):
    weights = [(1 << 20) // math.isqrt(rank ** skew) + 1 for rank in range(2, number_of + 1)]
    spare, given = total - most - (number_of - 1), [1] * (number_of - 1)
    while spare > 0:
        candidates = [i for i in range(number_of - 1) if given[i] < most]
        pool, budget = sum([weights[i] for i in candidates]), spare
        for i in candidates:
            extra = min(most - given[i], max(1, budget * weights[i] // pool), spare)
            given[i] = given[i] + extra
            spare = spare - extra
    return np.array([most] + given)


def uneven(own_key, number_of, total, limit, lean):
    if number_of == 2:
        one = jax.random.randint(own_key, (), max(1, total - limit), min(limit, total - 1) + 1)
        return jnp.stack([one, total - one])
    sizes = jnp.asarray(split_up(number_of, total, limit, lean), jnp.int32)
    pairs = (number_of - 1) // 2
    donor, sink = sizes[1:1 + 2 * pairs:2], sizes[2:2 + 2 * pairs:2]
    margin = jnp.minimum(donor - 1, limit - sink)
    passed = jax.random.randint(jax.random.fold_in(own_key, 1), (pairs,), 0, 1 << 20) % (margin + 1)
    sizes = sizes.at[1:1 + 2 * pairs:2].set(donor - passed).at[2:2 + 2 * pairs:2].set(sink + passed)
    return sizes[jax.random.permutation(jax.random.fold_in(own_key, 2), number_of)]


def scatter_about(stream_key, shape, spread, limit, cuts=(), kind=jnp.bfloat16):
    loudness = steps_of(stream_key, shape, cuts, -0.22, 0.18) if cuts else 1.0
    array = jax.random.normal(stream_key, shape, jnp.float32) * spread * loudness
    return jnp.minimum(jnp.maximum(array, -limit), limit).astype(kind)


def setup_inputs(seed: int = 0) -> dict:
    splits = jax.random.split(jax.random.key(seed), 9)
    events = scatter_about(splits[0], (TOKENS, D), 1.0, 6.0, ((0, 64),))
    in_proj = draw_in_proj(jax.random.fold_in(splits[8], 71), 0)
    out_proj = scatter_about(splits[2], (HEADS, DH, D), DH ** -0.5, 1.0, ((0, 16),))
    lengths = jax.vmap(lambda own: uneven(own, SEQS_DEV, TOK_DEV, MAXLEN, 2))(jax.random.split(splits[3], GROUPS)).reshape((GROUPS, SEQS_DEV)).astype(jnp.int32)
    targets = scatter_about(splits[4], (TOKENS, D), 1.0, 6.0, ((0, 64),))
    item_table = scatter_about(splits[5], (ITEMS, D), 1.0, 6.0, ((0, 1024),))
    sample_ids = draw_sample_ids(jax.random.fold_in(splits[8], 71), 0)
    sample_counts = place_ends(jax.random.randint(splits[7], (NSAMP,), 1, 65), jax.random.fold_in(splits[7], 1), 1, 64).astype(jnp.int32)
    return {"events": events, "in_proj": in_proj, "out_proj": out_proj, "lengths": lengths, "targets": targets, "item_table": item_table, "sample_ids": sample_ids, "sample_counts": sample_counts}


INV_TEMP = 20.0
EPSILON = 1e-06

def unit_rows(values):
    inv_norm = lax.rsqrt(lax.optimization_barrier(jnp.mean(values * values, -1, keepdims=True)) + EPSILON) / math.sqrt(values.shape[-1])
    return (values * inv_norm, inv_norm)

def sequence_mask(lengths_row, row_total):
    seq_ends = jnp.cumsum(lengths_row.astype(jnp.int32))
    positions = jnp.arange(row_total, dtype=jnp.int32)
    segment = lax.optimization_barrier(jnp.sum((positions[:, None] >= seq_ends[None, :]).astype(jnp.int32), 1))
    same_seq = segment[:, None] == segment[None, :]
    causal = positions[None, :] <= positions[:, None]
    return same_seq & causal

def pointwise_attention(normed, in_weight, lengths_row):
    row_total = normed.shape[0]
    model_width = normed.shape[1]
    heads_here = in_weight.shape[1]
    head_dim = in_weight.shape[2] // 4
    projected = jax.nn.silu(jnp.dot(normed, in_weight.reshape(model_width, -1), preferred_element_type=jnp.float32))
    projected = projected.reshape(row_total, heads_here, 4, head_dim)
    gate_part = projected[:, :, 0]
    value_part = projected[:, :, 1].astype(jnp.bfloat16)
    query_part = projected[:, :, 2].astype(jnp.bfloat16)
    key_part = projected[:, :, 3].astype(jnp.bfloat16)
    scores = jnp.einsum('thd,shd->hts', query_part.astype(jnp.float32), key_part.astype(jnp.float32))
    seq_mask = sequence_mask(lengths_row, row_total)
    weights = (jnp.where(seq_mask[None], jax.nn.silu(scores), 0.0) / MAXLEN).astype(jnp.bfloat16)
    attended = jnp.einsum('hts,shd->thd', weights.astype(jnp.float32), value_part.astype(jnp.float32))
    return (attended.reshape(row_total, -1), gate_part.reshape(row_total, -1))

def reference(events, in_proj, out_proj, lengths, targets, item_table, sample_ids, sample_counts):
    model_width = events.shape[1]
    sample_raw = jnp.take(item_table, sample_ids, axis=0).astype(jnp.float32)
    sample_unit, sample_inv = unit_rows(sample_raw)
    sample_bf = sample_unit.astype(jnp.bfloat16)
    log_counts = lax.optimization_barrier(jnp.log(sample_counts.astype(jnp.float32)).astype(jnp.bfloat16)).astype(jnp.float32)
    out_matrix = out_proj.reshape(-1, model_width)

    def group_step(item_acc, inputs):
        group_events, group_lengths, group_targets = inputs
        events_wide = group_events.astype(jnp.float32)
        normed = (events_wide * lax.rsqrt(lax.optimization_barrier(jnp.mean(events_wide * events_wide, -1, keepdims=True)) + EPSILON)).astype(jnp.bfloat16)
        attended, gate_part = pointwise_attention(normed, in_proj, group_lengths)
        row_mean = lax.optimization_barrier(jnp.mean(attended, -1, keepdims=True))
        row_var = jnp.maximum(lax.optimization_barrier(jnp.mean(attended * attended, -1, keepdims=True)) - row_mean * row_mean, 0.0)
        att_normed = (attended - row_mean) * lax.rsqrt(row_var + EPSILON)
        mixed_in = (att_normed * gate_part).astype(jnp.bfloat16)
        output_rows = events_wide + jnp.dot(mixed_in, out_matrix, preferred_element_type=jnp.float32)
        user_unit, user_inv = unit_rows(output_rows)
        user_bf = user_unit.astype(jnp.bfloat16)
        target_unit, target_inv = unit_rows(group_targets.astype(jnp.float32))
        positive = INV_TEMP * lax.optimization_barrier(jnp.sum(user_bf.astype(jnp.float32) * target_unit, -1))
        negative = INV_TEMP * jnp.dot(user_bf, sample_bf.T, preferred_element_type=jnp.float32) - log_counts[None, :]
        neg_exp = jnp.exp(negative)
        denom_total = jnp.exp(positive) + lax.optimization_barrier(jnp.sum(neg_exp, -1))
        loss_rows = jnp.log(denom_total) - positive
        neg_probs = (neg_exp / denom_total[:, None]).astype(jnp.bfloat16)
        pos_prob = jnp.exp(positive) / denom_total
        user_grad = INV_TEMP * (jnp.dot(neg_probs, sample_bf, preferred_element_type=jnp.float32) + (pos_prob - 1.0)[:, None] * target_unit)
        out_grad = user_inv * (user_grad - user_unit * lax.optimization_barrier(jnp.sum(user_unit * user_grad, -1, keepdims=True)))
        item_term = jnp.dot(neg_probs.T, user_bf, preferred_element_type=jnp.float32)
        return (item_acc + item_term, (loss_rows, out_grad))
    initial = jnp.zeros((NSAMP, model_width), jnp.float32)
    item_sum, (loss_rows, out_grads) = lax.scan(group_step, initial, (events.reshape(GROUPS, TOK_DEV, model_width), lengths, targets.reshape(GROUPS, TOK_DEV, model_width)))
    item_grad = INV_TEMP * item_sum
    d_samples = sample_inv * (item_grad - sample_unit * lax.optimization_barrier(jnp.sum(sample_unit * item_grad, -1, keepdims=True)))
    return (loss_rows.reshape(-1), out_grads.reshape(-1, model_width), d_samples)
```

```python
import functools
import math

import jax
import jax.numpy as jnp
from jax import lax
from jax.experimental import pallas as pl
from jax.experimental.pallas import tpu as pltpu
from jax.sharding import Mesh
from jax.sharding import PartitionSpec as P

MAXLEN = 256
INV_TEMP = 20.0
EPSILON = 1e-06
F32 = jnp.float32
BF16 = jnp.bfloat16
STAT_ROWS = 16
VMEM_LIMIT = 40 * 1024 * 1024


def dot(a, b, dims=((1,), (0,))):
    return lax.dot_general(a, b, (dims, ((), ())), preferred_element_type=F32)


def silu(x):
    return x / (1.0 + jnp.exp(-x))


def split3(x):
    hi = x.astype(BF16).astype(F32)
    mid = (x - hi).astype(BF16).astype(F32)
    return hi, mid, x - hi - mid


def unit_rows(values):
    inv_norm = lax.rsqrt(jnp.mean(values * values, -1, keepdims=True) + EPSILON) / math.sqrt(
        values.shape[-1]
    )
    return (values * inv_norm, inv_norm)


def to_columns(rows):
    n = rows[0].shape[1]
    at = lax.broadcasted_iota(jnp.int32, (128, n), 0)
    block = jnp.broadcast_to(rows[-1], (128, n))
    for k in range(len(rows) - 1):
        block = jnp.where(at == k, rows[k], block)
    return block.T


def attention_kernel(lengths, events, weight, out_proj, payload):
    n = events.shape[0]
    dh = out_proj.shape[0]
    wide = events[...].astype(F32)
    normed = (wide * lax.rsqrt(jnp.mean(wide * wide, -1, keepdims=True) + EPSILON)).astype(BF16)
    proj = silu(dot(normed, weight[...]))
    turned = proj.T
    gate = turned[:dh]
    value = turned[dh : 2 * dh].astype(BF16)
    query = turned[2 * dh : 3 * dh].astype(BF16)
    key = proj[:, 3 * dh :].astype(BF16)
    scores = dot(key, query)
    position = lax.broadcasted_iota(jnp.int32, (1, n), 1)
    first = jnp.zeros((1, n), jnp.int32)
    end = jnp.int32(0)
    for k in range(lengths.shape[1]):
        end = end + lengths[0, k]
        first = jnp.where(position >= end, end, first)
    j_at = lax.broadcasted_iota(jnp.int32, (n, n), 0)
    seen = (j_at <= position) & (j_at >= first)
    weights = (jnp.where(seen, silu(scores), 0.0) / MAXLEN).astype(BF16)
    attended = dot(value, weights)
    sums = split3(jnp.sum(attended, 0, keepdims=True))
    squares = split3(jnp.sum(attended * attended, 0, keepdims=True))
    at = lax.broadcasted_iota(jnp.int32, (STAT_ROWS, n), 0)
    stats = jnp.zeros((STAT_ROWS, n), F32)
    for k, row in enumerate(sums + squares):
        stats = jnp.where(at == k, row, stats)
    payload[0:dh, :] = (attended * gate).astype(BF16)
    payload[dh : 2 * dh, :] = gate.astype(BF16)
    payload[2 * dh : 2 * dh + STAT_ROWS, :] = stats.astype(BF16)
    payload[2 * dh + STAT_ROWS :, :] = out_proj[...]


def score_kernel(
    heads, share, me, gathered, events, targets, samples,
    exps, sums, positive_row, user_bf, user_part, own_out, out_rows,
):
    width = events.shape[1]
    n = events.shape[0]
    step = gathered.shape[0] // heads
    dh = (step - STAT_ROWS) // 3

    def part(lo, hi):
        return jnp.concatenate([gathered[h * step + lo : h * step + hi, :] for h in range(heads)], 0)

    stats = jnp.zeros((STAT_ROWS, n), F32)
    for h in range(heads):
        stats = stats + gathered[h * step + 2 * dh : h * step + 2 * dh + STAT_ROWS, :].astype(F32)
    full = heads * dh
    row_mean = (stats[0:1] + stats[1:2] + stats[2:3]) / full
    row_sq = (stats[3:4] + stats[4:5] + stats[5:6]) / full
    scale = lax.rsqrt(jnp.maximum(row_sq - row_mean * row_mean, 0.0) + EPSILON)
    cols = to_columns([scale, scale * row_mean])
    matrix = part(2 * dh + STAT_ROWS, step)
    mixed = cols[:, 0:1] * dot(part(0, dh), matrix, ((0,), (0,))) - cols[:, 1:2] * dot(
        part(dh, 2 * dh), matrix, ((0,), (0,))
    )
    output = events[...].astype(F32) + mixed
    out_rows[...] = output
    own_out[...] = out_rows[pl.ds(pl.multiple_of(me[0] * share, share), share), :]
    unit, _ = unit_rows(output)
    rounded = unit.astype(BF16)
    user_bf[...] = rounded
    target_unit, _ = unit_rows(targets[...].astype(F32))
    positive = INV_TEMP * jnp.sum(rounded.astype(F32) * target_unit, -1, keepdims=True)
    positive_row[...] = jnp.broadcast_to(positive, (n, 128)).T[0:8]
    sample_bf = samples[:, :width]
    log_counts = samples[:, width : width + 128].astype(F32)[:, 0:1]
    neg_exp = jnp.exp(INV_TEMP * dot(sample_bf, rounded, ((1,), (1,))) - log_counts)
    exps[...] = neg_exp
    sums[...] = jnp.broadcast_to(jnp.sum(neg_exp, 0, keepdims=True), sums.shape)
    user_part[...] = dot(neg_exp.astype(BF16), sample_bf, ((0,), (0,))).astype(BF16)


def item_kernel(share, me, sums, positive_row, exps, user_bf, loss, item_part, own_cols, all_cols):
    positive = positive_row[0:1]
    pos_exp = jnp.exp(positive)
    total = pos_exp + jnp.sum(sums[...], 0, keepdims=True)
    loss[...] = jnp.log(total) - positive
    probs = (exps[...] / total).astype(BF16)
    item_part[...] = dot(probs, user_bf[...])
    all_cols[...] = to_columns([1.0 / total, pos_exp / total - 1.0])
    own_cols[...] = all_cols[pl.ds(pl.multiple_of(me[0] * share, share), share), :]


def final_kernel(item_recv, own_raw, user_recv, own_cols, own_out, own_targets, d_user, d_samples):
    slots = own_raw.shape[0]
    share = own_out.shape[0]
    item_sum = item_recv[0:slots, :]
    for k in range(1, item_recv.shape[0] // slots):
        item_sum = item_sum + item_recv[k * slots : (k + 1) * slots, :]
    own_unit, own_inv = unit_rows(own_raw[...])
    item_grad = INV_TEMP * item_sum
    d_samples[...] = own_inv * (
        item_grad - own_unit * jnp.sum(own_unit * item_grad, -1, keepdims=True)
    )
    user_part = user_recv[0:share, :].astype(F32) + user_recv[share:, :].astype(F32)
    user_unit, user_inv = unit_rows(own_out[...])
    target_unit, _ = unit_rows(own_targets[...].astype(F32))
    user_grad = INV_TEMP * (user_part * own_cols[:, 0:1] + own_cols[:, 1:2] * target_unit)
    d_user[...] = user_inv * (
        user_grad - user_unit * jnp.sum(user_unit * user_grad, -1, keepdims=True)
    )


def call(kernel, outs, scalars, *args, scratch=()):
    smem = pl.BlockSpec(memory_space=pltpu.SMEM)
    vmem = pl.BlockSpec(memory_space=pltpu.VMEM)
    return pl.pallas_call(
        kernel,
        out_shape=[jax.ShapeDtypeStruct(s, t) for s, t in outs],
        in_specs=[smem] * len(scalars) + [vmem] * len(args),
        out_specs=[vmem] * len(outs),
        scratch_shapes=list(scratch),
        compiler_params=pltpu.CompilerParams(vmem_limit_bytes=VMEM_LIMIT),
    )(*scalars, *args)


def per_device(events, in_proj, out_proj, lengths, targets, item_table, sample_ids, sample_counts):
    n, width = events.shape
    dh = out_proj.shape[1]
    heads = lax.axis_size(("z", "c"))
    groups = lax.axis_size(("y", "x"))
    slots = sample_ids.shape[0]
    scored = slots * groups
    share = n // heads
    me = lax.axis_index(("z", "c"))
    me_ref = me.astype(jnp.int32).reshape(1)

    (payload,) = call(
        attention_kernel,
        [((3 * dh + STAT_ROWS, n), BF16)],
        [lengths],
        events,
        in_proj.reshape(width, -1),
        out_proj.reshape(dh, width),
    )
    payload, sample_ids = lax.optimization_barrier((payload, sample_ids))
    gathered = lax.all_gather(payload, ("z", "c"), axis=0, tiled=True)

    local_rows = jnp.remainder(sample_ids, item_table.shape[0])
    own_raw = jnp.take(item_table, local_rows, axis=0).astype(F32)
    own_unit, _ = unit_rows(own_raw)
    own_log = jnp.log(sample_counts.astype(F32)).astype(BF16)
    own_pack = jnp.concatenate(
        [own_unit.astype(BF16), jnp.broadcast_to(own_log[:, None], (slots, 128))], 1
    )
    samples = lax.all_to_all(
        jnp.tile(own_pack, (groups, 1)), ("y", "x"), 0, 0, tiled=True
    )

    exps, sums, positive_row, user_bf, user_part, own_out = call(
        functools.partial(score_kernel, heads, share),
        [
            ((scored, n), F32),
            ((heads, n), F32),
            ((8, n), F32),
            ((n, width), BF16),
            ((n, width), BF16),
            ((share, width), F32),
        ],
        [me_ref],
        gathered,
        events,
        targets,
        samples,
        scratch=[pltpu.VMEM((n, width), F32)],
    )
    user_over_z = lax.psum_scatter(user_part, "z", scatter_dimension=0, tiled=True)
    all_sums = lax.all_to_all(sums, ("z", "c"), 0, 0, tiled=True)
    loss, item_part, own_cols = call(
        functools.partial(item_kernel, share),
        [((1, n), F32), ((scored, width), F32), ((share, 128), F32)],
        [me_ref],
        all_sums,
        positive_row,
        exps,
        user_bf,
        scratch=[pltpu.VMEM((n, 128), F32)],
    )
    item_recv = lax.all_to_all(item_part, ("y", "x"), 0, 0, tiled=True)
    item_recv, user_over_z = lax.optimization_barrier((item_recv, user_over_z))
    user_recv = lax.all_to_all(user_over_z, "c", 0, 0, tiled=True)
    own_targets = lax.dynamic_slice_in_dim(targets, me * share, share, 0)
    d_user, d_samples = call(
        final_kernel,
        [((share, width), F32), ((slots, width), F32)],
        [],
        item_recv,
        own_raw,
        user_recv,
        own_cols,
        own_out,
        own_targets,
    )
    return (loss.reshape(-1), d_user, d_samples)


def solution(mesh):
    side = math.isqrt(mesh.shape["dp"])
    cores = 2
    devices = mesh.devices.reshape(mesh.shape["dp"] // side, side, mesh.shape["mp"] // cores, cores)
    fine = Mesh(devices, ("y", "x", "z", "c"))
    dp, mp, both = ("y", "x"), ("z", "c"), ("y", "x", "z", "c")
    placed = (
        P(dp, None),
        P(None, mp, None),
        P(mp, None, None),
        P(dp, None),
        P(dp, None),
        P(both, None),
        P(both),
        P(both),
    )
    return jax.shard_map(
        per_device,
        mesh=fine,
        in_specs=placed,
        out_specs=(P(dp), P(both, None), P(both, None)),
        check_vma=False,
    )
```

```python
import functools
import math

import jax
import jax.numpy as jnp
from jax import lax
from jax.experimental import pallas as pl
from jax.experimental.pallas import tpu as pltpu
from jax.sharding import PartitionSpec as P

MAXLEN = 256
INV_TEMP = 20.0
EPSILON = 1e-06
F32 = jnp.float32
BF16 = jnp.bfloat16
STAT_ROWS = 8
SUM_ROWS = 8
FIRST_LIMIT = 62 * 1024 * 1024
VMEM_LIMIT = 40 * 1024 * 1024


def dot(a, b, dims=((1,), (0,))):
    return lax.dot_general(a, b, (dims, ((), ())), preferred_element_type=F32)


def silu(x):
    return x / (1.0 + jnp.exp(-x))


def split3(x):
    hi = x.astype(BF16).astype(F32)
    mid = (x - hi).astype(BF16).astype(F32)
    return hi, mid, x - hi - mid


def unit_rows(values):
    inv_norm = lax.rsqrt(jnp.mean(values * values, -1, keepdims=True) + EPSILON) / math.sqrt(
        values.shape[-1]
    )
    return (values * inv_norm, inv_norm)


def to_columns(rows):
    n = rows[0].shape[1]
    at = lax.broadcasted_iota(jnp.int32, (128, n), 0)
    block = jnp.broadcast_to(rows[-1], (128, n))
    for k in range(len(rows) - 1):
        block = jnp.where(at == k, rows[k], block)
    return block.T


def first_kernel(
    copies, ids_hbm, counts_hbm, lengths_hbm, table_hbm, events_hbm, weight_hbm, out_hbm,
    blocks, own_raw, gated, rest,
    ids, counts, lengths, table, events, weight, out_proj, sem,
):
    slots = own_raw.shape[0]
    count, width = table.shape
    n = events.shape[0]
    dh = out_proj.shape[0]
    loads = []
    for k, (source, target) in enumerate(
        [
            (ids_hbm, ids),
            (counts_hbm, counts),
            (lengths_hbm, lengths),
            (table_hbm, table),
            (events_hbm, events),
            (weight_hbm, weight),
            (out_hbm, out_proj),
        ]
    ):
        loads.append(pltpu.make_async_copy(source, target, sem.at[k]))
        loads[-1].start()

    loads[0].wait()
    loads[1].wait()
    slot = lax.broadcasted_iota(jnp.int32, (slots, count), 0)
    at = lax.broadcasted_iota(jnp.int32, (slots, count), 1)
    wanted = jnp.zeros((slots, count), jnp.int32)
    drawn = jnp.ones((slots, 128), jnp.int32)
    slot_narrow = lax.broadcasted_iota(jnp.int32, (slots, 128), 0)
    for k in range(slots):
        wanted = jnp.where(slot == k, lax.rem(ids[k], count), wanted)
        drawn = jnp.where(slot_narrow == k, counts[k], drawn)
    logs = jnp.log(drawn.astype(F32))
    loads[3].wait()
    raw = dot((at == wanted).astype(F32).astype(BF16), table[...])
    own_raw[...] = raw
    unit, _ = unit_rows(raw)
    pack = jnp.concatenate([unit, logs], 1)
    twice = jnp.concatenate([pack, pack], 0).astype(BF16)
    for k in range(copies // 2):
        blocks[2 * k * slots : 2 * (k + 1) * slots, :] = twice

    loads[2].wait()
    position = lax.broadcasted_iota(jnp.int32, (1, n), 1)
    first = jnp.zeros((1, n), jnp.int32)
    end = jnp.int32(0)
    for k in range(lengths.shape[1]):
        end = end + lengths[0, k]
        first = jnp.where(position >= end, end, first)
    j_at = lax.broadcasted_iota(jnp.int32, (n, n), 0)
    seen = (j_at <= position) & (j_at >= first)
    loads[4].wait()
    wide = events[...].astype(F32)
    normed = (wide * lax.rsqrt(jnp.mean(wide * wide, -1, keepdims=True) + EPSILON)).astype(BF16)
    loads[5].wait()
    proj = silu(dot(normed, weight[...]))
    turned = proj.T
    gate = turned[:dh]
    value = turned[dh : 2 * dh].astype(BF16)
    query = turned[2 * dh : 3 * dh].astype(BF16)
    key = proj[:, 3 * dh :].astype(BF16)
    scores = dot(key, query)
    weights = (jnp.where(seen, silu(scores), 0.0) / MAXLEN).astype(BF16)
    attended = dot(value, weights)
    sums = split3(jnp.sum(attended, 0, keepdims=True))
    squares = split3(jnp.sum(attended * attended, 0, keepdims=True))
    at = lax.broadcasted_iota(jnp.int32, (STAT_ROWS, n), 0)
    stats = jnp.zeros((STAT_ROWS, n), F32)
    for k, row in enumerate(sums + squares):
        stats = jnp.where(at == k, row, stats)
    half = dh // 2
    gated[0:dh, :] = (attended * gate).astype(BF16)
    gated[dh : dh + half, :] = gate[:half].astype(BF16)
    gated[dh + half :, :] = stats.astype(BF16)
    rest[dh:, :] = gate[half:].astype(BF16)
    loads[6].wait()
    rest[0:dh, :] = out_proj[...]


def score_kernel(
    share, me, gated, rest, events, targets, samples,
    exps, packed, positive_row, user_bf, own_out, own_targets, out_rows,
):
    n, width = events.shape
    heads = gated.shape[0]
    dh = rest.shape[1] * 2 // 3
    half = dh // 2
    stats = gated[0, dh + half :, :].astype(F32)
    for h in range(1, heads):
        stats = stats + gated[h, dh + half :, :].astype(F32)
    full = heads * dh
    row_mean = (stats[0:1] + stats[1:2] + stats[2:3]) / full
    row_sq = (stats[3:4] + stats[4:5] + stats[5:6]) / full
    scale = lax.rsqrt(jnp.maximum(row_sq - row_mean * row_mean, 0.0) + EPSILON)
    cols = to_columns([scale, scale * row_mean])
    products = jnp.concatenate([gated[h, :dh, :] for h in range(heads)], 0)
    gates = jnp.concatenate(
        [part for h in range(heads) for part in (gated[h, dh : dh + half, :], rest[h, dh:, :])], 0
    )
    matrix = jnp.concatenate([rest[h, :dh, :] for h in range(heads)], 0)
    mixed = cols[:, 0:1] * dot(products, matrix, ((0,), (0,))) - cols[:, 1:2] * dot(
        gates, matrix, ((0,), (0,))
    )
    output = events[...].astype(F32) + mixed
    out_rows[...] = output
    own = pl.ds(pl.multiple_of(me[0] * share, share), share)
    own_out[...] = out_rows[own, :]
    own_targets[...] = targets[own, :]
    unit, _ = unit_rows(output)
    rounded = unit.astype(BF16)
    user_bf[...] = rounded
    target_unit, _ = unit_rows(targets[...].astype(F32))
    positive = INV_TEMP * jnp.sum(rounded.astype(F32) * target_unit, -1, keepdims=True)
    positive_row[...] = jnp.broadcast_to(positive, (n, 128)).T[0:8]
    sample_bf = samples[:, :width]
    log_counts = samples[:, width : width + 128].astype(F32)[:, 0:1]
    neg_exp = jnp.exp(INV_TEMP * dot(sample_bf, rounded, ((1,), (1,))) - log_counts)
    exps[...] = neg_exp
    user_part = dot(neg_exp.astype(BF16), sample_bf, ((0,), (0,))).astype(BF16)
    at = lax.broadcasted_iota(jnp.int32, (SUM_ROWS, n), 0)
    sums = jnp.zeros((SUM_ROWS, n), F32)
    for k, row in enumerate(split3(jnp.sum(neg_exp, 0, keepdims=True))):
        sums = jnp.where(at == k, row, sums)
    sums = sums.astype(BF16)
    for h in range(heads):
        packed[h, 0:share, :] = user_part[h * share : (h + 1) * share]
        packed[h, share:, :] = sums


def grad_kernel(
    share, me, packed, positive_row, exps, user_bf,
    loss, item_part, own_user, own_cols, all_cols,
):
    positive = positive_row[0:1]
    pos_exp = jnp.exp(positive)
    user_sum = packed[0, 0:share, :].astype(F32)
    sums = packed[0, share:, :].astype(F32)
    for h in range(1, packed.shape[0]):
        user_sum = user_sum + packed[h, 0:share, :].astype(F32)
        sums = sums + packed[h, share:, :].astype(F32)
    own_user[...] = user_sum
    total = pos_exp + (sums[0:1] + sums[1:2] + sums[2:3])
    loss[...] = jnp.log(total) - positive
    probs = (exps[...] / total).astype(BF16)
    item_part[...] = dot(probs, user_bf[...])
    all_cols[...] = to_columns([1.0 / total, pos_exp / total - 1.0])
    own_cols[...] = all_cols[pl.ds(pl.multiple_of(me[0] * share, share), share), :]


def final_kernel(item_recv, own_raw, own_user, own_cols, own_out, own_targets, d_user, d_samples):
    slots = own_raw.shape[0]
    item_sum = item_recv[0:slots, :]
    for k in range(1, item_recv.shape[0] // slots):
        item_sum = item_sum + item_recv[k * slots : (k + 1) * slots, :]
    own_unit, own_inv = unit_rows(own_raw[...])
    item_grad = INV_TEMP * item_sum
    d_samples[...] = own_inv * (
        item_grad - own_unit * jnp.sum(own_unit * item_grad, -1, keepdims=True)
    )
    user_unit, user_inv = unit_rows(own_out[...])
    target_unit, _ = unit_rows(own_targets[...].astype(F32))
    user_grad = INV_TEMP * (own_user[...] * own_cols[:, 0:1] + own_cols[:, 1:2] * target_unit)
    d_user[...] = user_inv * (
        user_grad - user_unit * jnp.sum(user_unit * user_grad, -1, keepdims=True)
    )


def call(kernel, outs, scalars, *args, remote=(), scratch=(), limit=VMEM_LIMIT):
    smem = pl.BlockSpec(memory_space=pltpu.SMEM)
    vmem = pl.BlockSpec(memory_space=pltpu.VMEM)
    anywhere = pl.BlockSpec(memory_space=pl.ANY)
    return pl.pallas_call(
        kernel,
        out_shape=[jax.ShapeDtypeStruct(s, t) for s, t in outs],
        in_specs=[smem] * len(scalars) + [anywhere] * len(remote) + [vmem] * len(args),
        out_specs=[vmem] * len(outs),
        scratch_shapes=list(scratch),
        compiler_params=pltpu.CompilerParams(vmem_limit_bytes=limit),
    )(*scalars, *remote, *args)


def per_device(events, in_proj, out_proj, lengths, targets, item_table, sample_ids, sample_counts):
    n, width = events.shape
    dh = out_proj.shape[1]
    heads = lax.axis_size("mp")
    groups = lax.axis_size("dp")
    slots = sample_ids.shape[0]
    scored = slots * groups
    share = n // heads
    me = lax.axis_index("mp")
    me_ref = me.astype(jnp.int32).reshape(1)

    blocks, own_raw, gated, rest = call(
        functools.partial(first_kernel, groups),
        [
            ((scored, width + 128), BF16),
            ((slots, width), F32),
            ((dh + dh // 2 + STAT_ROWS, n), BF16),
            ((dh + dh // 2, width), BF16),
        ],
        [],
        remote=[
            sample_ids,
            sample_counts,
            lengths,
            item_table,
            events,
            in_proj.reshape(width, -1),
            out_proj.reshape(dh, width),
        ],
        scratch=[
            pltpu.SMEM(sample_ids.shape, jnp.int32),
            pltpu.SMEM(sample_counts.shape, jnp.int32),
            pltpu.SMEM(lengths.shape, jnp.int32),
            pltpu.VMEM(item_table.shape, BF16),
            pltpu.VMEM((n, width), BF16),
            pltpu.VMEM((width, 4 * dh), BF16),
            pltpu.VMEM((dh, width), BF16),
            pltpu.SemaphoreType.DMA((7,)),
        ],
        limit=FIRST_LIMIT,
    )
    samples = lax.all_to_all(blocks, "dp", 0, 0, tiled=True)
    gated = lax.all_gather(gated, "mp", axis=0)
    rest = lax.all_gather(rest, "mp", axis=0)

    exps, packed, positive_row, user_bf, own_out, own_targets = call(
        functools.partial(score_kernel, share),
        [
            ((scored, n), F32),
            ((heads, share + SUM_ROWS, n), BF16),
            ((8, n), F32),
            ((n, width), BF16),
            ((share, width), F32),
            ((share, width), BF16),
        ],
        [me_ref],
        gated,
        rest,
        events,
        targets,
        samples,
        scratch=[pltpu.VMEM((n, width), F32)],
    )
    packed = lax.all_to_all(packed, "mp", 0, 0, tiled=True)
    loss, item_part, own_user, own_cols = call(
        functools.partial(grad_kernel, share),
        [((1, n), F32), ((scored, width), F32), ((share, width), F32), ((share, 128), F32)],
        [me_ref],
        packed,
        positive_row,
        exps,
        user_bf,
        scratch=[pltpu.VMEM((n, 128), F32)],
    )
    item_recv = lax.all_to_all(item_part, "dp", 0, 0, tiled=True)
    d_user, d_samples = call(
        final_kernel,
        [((share, width), F32), ((slots, width), F32)],
        [],
        item_recv,
        own_raw,
        own_user,
        own_cols,
        own_out,
        own_targets,
    )
    return (loss.reshape(-1), d_user, d_samples)


def solution(mesh):
    placed = (
        P("dp", None),
        P(None, "mp", None),
        P("mp", None, None),
        P("dp", None),
        P("dp", None),
        P(("dp", "mp"), None),
        P(("dp", "mp")),
        P(("dp", "mp")),
    )
    return jax.shard_map(
        per_device,
        mesh=mesh,
        in_specs=placed,
        out_specs=(P("dp"), P(("dp", "mp"), None), P(("dp", "mp"), None)),
        check_vma=False,
    )
```

```python
import functools
import math

import jax
import jax.numpy as jnp
from jax import lax
from jax.experimental import pallas as pl
from jax.experimental.pallas import tpu as pltpu
from jax.sharding import PartitionSpec as P

MAXLEN = 256
INV_TEMP = 20.0
EPSILON = 1e-06
F32 = jnp.float32
BF16 = jnp.bfloat16
STAT_ROWS = 8
FIRST_LIMIT = 62 * 1024 * 1024
VMEM_LIMIT = 40 * 1024 * 1024


def dot(a, b, dims=((1,), (0,))):
    return lax.dot_general(a, b, (dims, ((), ())), preferred_element_type=F32)


def silu(x):
    return x / (1.0 + jnp.exp(-x))


def split3(x):
    hi = x.astype(BF16).astype(F32)
    mid = (x - hi).astype(BF16).astype(F32)
    return hi, mid, x - hi - mid


def unit_rows(values):
    inv_norm = lax.rsqrt(jnp.mean(values * values, -1, keepdims=True) + EPSILON) / math.sqrt(
        values.shape[-1]
    )
    return (values * inv_norm, inv_norm)


def to_columns(rows):
    n = rows[0].shape[1]
    at = lax.broadcasted_iota(jnp.int32, (128, n), 0)
    block = jnp.broadcast_to(rows[-1], (128, n))
    for k in range(len(rows) - 1):
        block = jnp.where(at == k, rows[k], block)
    return block.T


def first_kernel(
    copies, ids_hbm, counts_hbm, lengths_hbm, table_hbm, events_hbm, weight_hbm, out_hbm,
    blocks, own_raw, gated, rest,
    ids, counts, lengths, table, events, weight, out_proj, sem,
):
    slots = own_raw.shape[0]
    count, width = table.shape
    n = events.shape[0]
    dh = out_proj.shape[0]
    loads = []
    for k, (source, target) in enumerate(
        [
            (ids_hbm, ids),
            (counts_hbm, counts),
            (lengths_hbm, lengths),
            (table_hbm, table),
            (events_hbm, events),
            (weight_hbm, weight),
            (out_hbm, out_proj),
        ]
    ):
        loads.append(pltpu.make_async_copy(source, target, sem.at[k]))
        loads[-1].start()

    loads[0].wait()
    loads[1].wait()
    slot = lax.broadcasted_iota(jnp.int32, (slots, count), 0)
    at = lax.broadcasted_iota(jnp.int32, (slots, count), 1)
    wanted = jnp.zeros((slots, count), jnp.int32)
    drawn = jnp.ones((slots, 128), jnp.int32)
    slot_narrow = lax.broadcasted_iota(jnp.int32, (slots, 128), 0)
    for k in range(slots):
        wanted = jnp.where(slot == k, lax.rem(ids[k], count), wanted)
        drawn = jnp.where(slot_narrow == k, counts[k], drawn)
    logs = jnp.log(drawn.astype(F32))
    loads[3].wait()
    raw = dot((at == wanted).astype(F32).astype(BF16), table[...])
    own_raw[...] = raw
    unit, _ = unit_rows(raw)
    pack = jnp.concatenate([unit, logs], 1)
    twice = jnp.concatenate([pack, pack], 0).astype(BF16)
    for k in range(copies // 2):
        blocks[2 * k * slots : 2 * (k + 1) * slots, :] = twice

    loads[2].wait()
    position = lax.broadcasted_iota(jnp.int32, (1, n), 1)
    first = jnp.zeros((1, n), jnp.int32)
    end = jnp.int32(0)
    for k in range(lengths.shape[1]):
        end = end + lengths[0, k]
        first = jnp.where(position >= end, end, first)
    j_at = lax.broadcasted_iota(jnp.int32, (n, n), 0)
    seen = (j_at <= position) & (j_at >= first)
    loads[4].wait()
    wide = events[...].astype(F32)
    normed = (wide * lax.rsqrt(jnp.mean(wide * wide, -1, keepdims=True) + EPSILON)).astype(BF16)
    loads[5].wait()
    proj = silu(dot(normed, weight[...]))
    turned = proj.T
    gate = turned[:dh]
    value = turned[dh : 2 * dh].astype(BF16)
    query = turned[2 * dh : 3 * dh].astype(BF16)
    key = proj[:, 3 * dh :].astype(BF16)
    scores = dot(key, query)
    weights = (jnp.where(seen, silu(scores), 0.0) / MAXLEN).astype(BF16)
    attended = dot(value, weights)
    sums = split3(jnp.sum(attended, 0, keepdims=True))
    squares = split3(jnp.sum(attended * attended, 0, keepdims=True))
    at = lax.broadcasted_iota(jnp.int32, (STAT_ROWS, n), 0)
    stats = jnp.zeros((STAT_ROWS, n), F32)
    for k, row in enumerate(sums + squares):
        stats = jnp.where(at == k, row, stats)
    half = dh // 2
    gated[0:dh, :] = (attended * gate).astype(BF16)
    gated[dh : dh + half, :] = gate[:half].astype(BF16)
    gated[dh + half :, :] = stats.astype(BF16)
    rest[dh:, :] = gate[half:].astype(BF16)
    loads[6].wait()
    rest[0:dh, :] = out_proj[...]


def score_kernel(
    share, me, gated, rest, events, targets, samples,
    exps, sums, positive_row, user_bf, keep, give, own_out, own_targets, out_rows,
):
    n, width = events.shape
    heads = gated.shape[0]
    dh = rest.shape[1] * 2 // 3
    half = dh // 2
    stats = gated[0, dh + half :, :].astype(F32)
    for h in range(1, heads):
        stats = stats + gated[h, dh + half :, :].astype(F32)
    full = heads * dh
    row_mean = (stats[0:1] + stats[1:2] + stats[2:3]) / full
    row_sq = (stats[3:4] + stats[4:5] + stats[5:6]) / full
    scale = lax.rsqrt(jnp.maximum(row_sq - row_mean * row_mean, 0.0) + EPSILON)
    cols = to_columns([scale, scale * row_mean])
    products = jnp.concatenate([gated[h, :dh, :] for h in range(heads)], 0)
    gates = jnp.concatenate(
        [part for h in range(heads) for part in (gated[h, dh : dh + half, :], rest[h, dh:, :])], 0
    )
    matrix = jnp.concatenate([rest[h, :dh, :] for h in range(heads)], 0)
    mixed = cols[:, 0:1] * dot(products, matrix, ((0,), (0,))) - cols[:, 1:2] * dot(
        gates, matrix, ((0,), (0,))
    )
    output = events[...].astype(F32) + mixed
    out_rows[...] = output
    own = pl.ds(pl.multiple_of(me[0] * share, share), share)
    own_out[...] = out_rows[own, :]
    own_targets[...] = targets[own, :]
    unit, _ = unit_rows(output)
    rounded = unit.astype(BF16)
    user_bf[...] = rounded
    target_unit, _ = unit_rows(targets[...].astype(F32))
    positive = INV_TEMP * jnp.sum(rounded.astype(F32) * target_unit, -1, keepdims=True)
    positive_row[...] = jnp.broadcast_to(positive, (n, 128)).T[0:8]
    sample_bf = samples[:, :width]
    log_counts = samples[:, width : width + 128].astype(F32)[:, 0:1]
    neg_exp = jnp.exp(INV_TEMP * dot(sample_bf, rounded, ((1,), (1,))) - log_counts)
    exps[...] = neg_exp
    user_part = dot(neg_exp.astype(BF16), sample_bf, ((0,), (0,))).astype(BF16)
    sums[...] = jnp.broadcast_to(jnp.sum(neg_exp, 0, keepdims=True)[None], sums.shape)
    first_core = lax.rem(me[0], 2) == 0
    for z in range(heads // 2):
        even = user_part[2 * z * share : (2 * z + 1) * share]
        odd = user_part[(2 * z + 1) * share : (2 * z + 2) * share]
        keep[z] = jnp.where(first_core, even, odd)
        give[z] = jnp.where(first_core, odd, even)


def grad_kernel(share, me, sums, positive_row, exps, user_bf, keep, got, *refs):
    chips = keep.shape[0]
    loss, item_part, own_cols = refs[:3]
    pieces = refs[3 : 3 + chips]
    all_cols, halves = refs[3 + chips :]
    positive = positive_row[0:1]
    pos_exp = jnp.exp(positive)
    for z in range(chips):
        halves[z] = (keep[z].astype(F32) + got[z].astype(F32)).astype(BF16)
    for hop in range(chips):
        pieces[hop][...] = halves[lax.rem(me[0] // 2 + hop, chips)]
    total = pos_exp
    for k in range(sums.shape[0]):
        total = total + sums[k]
    loss[...] = jnp.log(total) - positive
    probs = (exps[...] / total).astype(BF16)
    item_part[...] = dot(probs, user_bf[...])
    all_cols[...] = to_columns([1.0 / total, pos_exp / total - 1.0])
    own_cols[...] = all_cols[pl.ds(pl.multiple_of(me[0] * share, share), share), :]


def final_kernel(item_recv, own_raw, own_cols, own_out, own_targets, *refs):
    user_parts, (d_user, d_samples) = refs[:-2], refs[-2:]
    slots = own_raw.shape[0]
    item_sum = item_recv[0:slots, :]
    for k in range(1, item_recv.shape[0] // slots):
        item_sum = item_sum + item_recv[k * slots : (k + 1) * slots, :]
    own_unit, own_inv = unit_rows(own_raw[...])
    item_grad = INV_TEMP * item_sum
    d_samples[...] = own_inv * (
        item_grad - own_unit * jnp.sum(own_unit * item_grad, -1, keepdims=True)
    )
    user_unit, user_inv = unit_rows(own_out[...])
    target_unit, _ = unit_rows(own_targets[...].astype(F32))
    user_part = user_parts[0][...].astype(F32)
    for part in user_parts[1:]:
        user_part = user_part + part[...].astype(F32)
    user_grad = INV_TEMP * (user_part * own_cols[:, 0:1] + own_cols[:, 1:2] * target_unit)
    d_user[...] = user_inv * (
        user_grad - user_unit * jnp.sum(user_unit * user_grad, -1, keepdims=True)
    )


def call(kernel, outs, scalars, *args, remote=(), scratch=(), limit=VMEM_LIMIT):
    smem = pl.BlockSpec(memory_space=pltpu.SMEM)
    vmem = pl.BlockSpec(memory_space=pltpu.VMEM)
    anywhere = pl.BlockSpec(memory_space=pl.ANY)
    return pl.pallas_call(
        kernel,
        out_shape=[jax.ShapeDtypeStruct(s, t) for s, t in outs],
        in_specs=[smem] * len(scalars) + [anywhere] * len(remote) + [vmem] * len(args),
        out_specs=[vmem] * len(outs),
        scratch_shapes=list(scratch),
        compiler_params=pltpu.CompilerParams(vmem_limit_bytes=limit),
    )(*scalars, *remote, *args)


def per_device(events, in_proj, out_proj, lengths, targets, item_table, sample_ids, sample_counts):
    n, width = events.shape
    dh = out_proj.shape[1]
    heads = lax.axis_size("mp")
    groups = lax.axis_size("dp")
    slots = sample_ids.shape[0]
    scored = slots * groups
    share = n // heads
    me = lax.axis_index("mp")
    me_ref = me.astype(jnp.int32).reshape(1)

    blocks, own_raw, gated, rest = call(
        functools.partial(first_kernel, groups),
        [
            ((scored, width + 128), BF16),
            ((slots, width), F32),
            ((dh + dh // 2 + STAT_ROWS, n), BF16),
            ((dh + dh // 2, width), BF16),
        ],
        [],
        remote=[
            sample_ids,
            sample_counts,
            lengths,
            item_table,
            events,
            in_proj.reshape(width, -1),
            out_proj.reshape(dh, width),
        ],
        scratch=[
            pltpu.SMEM(sample_ids.shape, jnp.int32),
            pltpu.SMEM(sample_counts.shape, jnp.int32),
            pltpu.SMEM(lengths.shape, jnp.int32),
            pltpu.VMEM(item_table.shape, BF16),
            pltpu.VMEM((n, width), BF16),
            pltpu.VMEM((width, 4 * dh), BF16),
            pltpu.VMEM((dh, width), BF16),
            pltpu.SemaphoreType.DMA((7,)),
        ],
        limit=FIRST_LIMIT,
    )
    samples = lax.all_to_all(blocks, "dp", 0, 0, tiled=True)
    gated = lax.all_gather(gated, "mp", axis=0)
    rest = lax.all_gather(rest, "mp", axis=0)

    chips = heads // 2
    exps, sums, positive_row, user_bf, keep, give, own_out, own_targets = call(
        functools.partial(score_kernel, share),
        [
            ((scored, n), F32),
            ((heads, 1, n), F32),
            ((8, n), F32),
            ((n, width), BF16),
            ((chips, share, width), BF16),
            ((chips, share, width), BF16),
            ((share, width), F32),
            ((share, width), BF16),
        ],
        [me_ref],
        gated,
        rest,
        events,
        targets,
        samples,
        scratch=[pltpu.VMEM((n, width), F32)],
    )
    got = lax.ppermute(give, "mp", [(k, k ^ 1) for k in range(heads)])
    sums = lax.all_to_all(sums, "mp", 0, 0, tiled=True)
    loss, item_part, own_cols, *pieces = call(
        functools.partial(grad_kernel, share),
        [((1, n), F32), ((scored, width), F32), ((share, 128), F32)]
        + [((share, width), BF16)] * chips,
        [me_ref],
        sums,
        positive_row,
        exps,
        user_bf,
        keep,
        got,
        scratch=[pltpu.VMEM((n, 128), F32), pltpu.VMEM((chips, share, width), BF16)],
    )
    item_recv = lax.all_to_all(item_part, "dp", 0, 0, tiled=True)
    pieces = pieces[:1] + [
        lax.ppermute(pieces[hop], "mp", [(k, (k + 2 * hop) % heads) for k in range(heads)])
        for hop in range(1, chips)
    ]
    d_user, d_samples = call(
        final_kernel,
        [((share, width), F32), ((slots, width), F32)],
        [],
        item_recv,
        own_raw,
        own_cols,
        own_out,
        own_targets,
        *pieces,
    )
    return (loss.reshape(-1), d_user, d_samples)


def solution(mesh):
    placed = (
        P("dp", None),
        P(None, "mp", None),
        P("mp", None, None),
        P("dp", None),
        P("dp", None),
        P(("dp", "mp"), None),
        P(("dp", "mp")),
        P(("dp", "mp")),
    )
    return jax.shard_map(
        per_device,
        mesh=mesh,
        in_specs=placed,
        out_specs=(P("dp"), P(("dp", "mp"), None), P(("dp", "mp"), None)),
        check_vma=False,
    )
```

```python
import functools
import math

import jax
import jax.numpy as jnp
from jax import lax
from jax.experimental import pallas as pl
from jax.experimental.pallas import tpu as pltpu
from jax.sharding import PartitionSpec as P

MAXLEN = 256
INV_TEMP = 20.0
EPSILON = 1e-06
F32 = jnp.float32
BF16 = jnp.bfloat16
STAT_ROWS = 8
FIRST_LIMIT = 62 * 1024 * 1024
VMEM_LIMIT = 40 * 1024 * 1024


def dot(a, b, dims=((1,), (0,))):
    return lax.dot_general(a, b, (dims, ((), ())), preferred_element_type=F32)


def silu(x):
    return x / (1.0 + jnp.exp(-x))


def split3(x):
    hi = x.astype(BF16).astype(F32)
    mid = (x - hi).astype(BF16).astype(F32)
    return hi, mid, x - hi - mid


def unit_rows(values):
    inv_norm = lax.rsqrt(jnp.mean(values * values, -1, keepdims=True) + EPSILON) / math.sqrt(
        values.shape[-1]
    )
    return (values * inv_norm, inv_norm)


def to_columns(rows):
    n = rows[0].shape[1]
    at = lax.broadcasted_iota(jnp.int32, (128, n), 0)
    block = jnp.broadcast_to(rows[-1], (128, n))
    for k in range(len(rows) - 1):
        block = jnp.where(at == k, rows[k], block)
    return block.T


def first_kernel(
    copies, ids_hbm, counts_hbm, lengths_hbm, table_hbm, events_hbm, weight_hbm, out_hbm,
    blocks, own_raw, gated, rest,
    ids, counts, lengths, table, events, weight, out_proj, sem,
):
    slots = own_raw.shape[0]
    count, width = table.shape
    n = events.shape[0]
    dh = out_proj.shape[0]
    loads = []
    for k, (source, target) in enumerate(
        [
            (ids_hbm, ids),
            (counts_hbm, counts),
            (lengths_hbm, lengths),
            (table_hbm, table),
            (events_hbm, events),
            (weight_hbm, weight),
            (out_hbm, out_proj),
        ]
    ):
        loads.append(pltpu.make_async_copy(source, target, sem.at[k]))
        loads[-1].start()

    loads[0].wait()
    loads[1].wait()
    slot = lax.broadcasted_iota(jnp.int32, (slots, count), 0)
    at = lax.broadcasted_iota(jnp.int32, (slots, count), 1)
    wanted = jnp.zeros((slots, count), jnp.int32)
    drawn = jnp.ones((slots, 128), jnp.int32)
    slot_narrow = lax.broadcasted_iota(jnp.int32, (slots, 128), 0)
    for k in range(slots):
        wanted = jnp.where(slot == k, lax.rem(ids[k], count), wanted)
        drawn = jnp.where(slot_narrow == k, counts[k], drawn)
    logs = jnp.log(drawn.astype(F32))
    loads[3].wait()
    raw = dot((at == wanted).astype(F32).astype(BF16), table[...])
    own_raw[...] = raw
    unit, _ = unit_rows(raw)
    pack = jnp.concatenate([unit, logs], 1)
    twice = jnp.concatenate([pack, pack], 0).astype(BF16)
    for k in range(copies // 2):
        blocks[2 * k * slots : 2 * (k + 1) * slots, :] = twice

    loads[2].wait()
    position = lax.broadcasted_iota(jnp.int32, (1, n), 1)
    first = jnp.zeros((1, n), jnp.int32)
    end = jnp.int32(0)
    for k in range(lengths.shape[1]):
        end = end + lengths[0, k]
        first = jnp.where(position >= end, end, first)
    j_at = lax.broadcasted_iota(jnp.int32, (n, n), 0)
    seen = (j_at <= position) & (j_at >= first)
    loads[4].wait()
    wide = events[...].astype(F32)
    normed = (wide * lax.rsqrt(jnp.mean(wide * wide, -1, keepdims=True) + EPSILON)).astype(BF16)
    loads[5].wait()
    proj = silu(dot(normed, weight[...]))
    turned = proj.T
    gate = turned[:dh]
    value = turned[dh : 2 * dh].astype(BF16)
    query = turned[2 * dh : 3 * dh].astype(BF16)
    key = proj[:, 3 * dh :].astype(BF16)
    scores = dot(key, query)
    weights = (jnp.where(seen, silu(scores), 0.0) / MAXLEN).astype(BF16)
    attended = dot(value, weights)
    sums = split3(jnp.sum(attended, 0, keepdims=True))
    squares = split3(jnp.sum(attended * attended, 0, keepdims=True))
    at = lax.broadcasted_iota(jnp.int32, (STAT_ROWS, n), 0)
    stats = jnp.zeros((STAT_ROWS, n), F32)
    for k, row in enumerate(sums + squares):
        stats = jnp.where(at == k, row, stats)
    half = dh // 2
    gated[0:dh, :] = (attended * gate).astype(BF16)
    gated[dh : dh + half, :] = gate[:half].astype(BF16)
    gated[dh + half :, :] = stats.astype(BF16)
    rest[dh:, :] = gate[half:].astype(BF16)
    loads[6].wait()
    rest[0:dh, :] = out_proj[...]


def score_kernel(
    share, me, gated, rest, events, targets, samples,
    exps, sums, positive_row, user_bf, keep, give, own_out, own_targets, out_rows,
):
    n, width = events.shape
    heads = gated.shape[0]
    dh = rest.shape[1] * 2 // 3
    half = dh // 2
    stats = gated[0, dh + half :, :].astype(F32)
    for h in range(1, heads):
        stats = stats + gated[h, dh + half :, :].astype(F32)
    full = heads * dh
    row_mean = (stats[0:1] + stats[1:2] + stats[2:3]) / full
    row_sq = (stats[3:4] + stats[4:5] + stats[5:6]) / full
    scale = lax.rsqrt(jnp.maximum(row_sq - row_mean * row_mean, 0.0) + EPSILON)
    cols = to_columns([scale, scale * row_mean])
    products = jnp.concatenate([gated[h, :dh, :] for h in range(heads)], 0)
    gates = jnp.concatenate(
        [part for h in range(heads) for part in (gated[h, dh : dh + half, :], rest[h, dh:, :])], 0
    )
    matrix = jnp.concatenate([rest[h, :dh, :] for h in range(heads)], 0)
    mixed = cols[:, 0:1] * dot(products, matrix, ((0,), (0,))) - cols[:, 1:2] * dot(
        gates, matrix, ((0,), (0,))
    )
    output = events[...].astype(F32) + mixed
    out_rows[...] = output
    own = pl.ds(pl.multiple_of(me[0] * share, share), share)
    own_out[...] = out_rows[own, :]
    own_targets[...] = targets[own, :]
    unit, _ = unit_rows(output)
    rounded = unit.astype(BF16)
    user_bf[...] = rounded
    target_unit, _ = unit_rows(targets[...].astype(F32))
    positive = INV_TEMP * jnp.sum(rounded.astype(F32) * target_unit, -1, keepdims=True)
    positive_row[...] = jnp.broadcast_to(positive, (n, 128)).T[0:8]
    sample_bf = samples[:, :width]
    log_counts = samples[:, width : width + 128].astype(F32)[:, 0:1]
    neg_exp = jnp.exp(INV_TEMP * dot(sample_bf, rounded, ((1,), (1,))) - log_counts)
    exps[...] = neg_exp
    user_part = dot(neg_exp.astype(BF16), sample_bf, ((0,), (0,))).astype(BF16)
    sums[...] = jnp.broadcast_to(jnp.sum(neg_exp, 0, keepdims=True)[None], sums.shape)
    first_core = lax.rem(me[0], 2) == 0
    for z in range(heads // 2):
        even = user_part[2 * z * share : (2 * z + 1) * share]
        odd = user_part[(2 * z + 1) * share : (2 * z + 2) * share]
        keep[z] = jnp.where(first_core, even, odd)
        give[z] = jnp.where(first_core, odd, even)


def halve_kernel(me, keep, got, own, other):
    chips = keep.shape[0]
    half = chips // 2
    z = me[0] // 2
    for hop in range(half):
        for target, far in ((own, 0), (other, half)):
            at = lax.rem(z + hop + far, chips)
            target[hop] = (keep[at].astype(F32) + got[at].astype(F32)).astype(BF16)


def add_kernel(own, got, *pieces):
    for hop in range(len(pieces)):
        pieces[hop][...] = (own[hop].astype(F32) + got[hop].astype(F32)).astype(BF16)


def grad_kernel(share, me, sums, positive_row, exps, user_bf, loss, item_part, own_cols, all_cols):
    slots = item_part.shape[1]
    positive = positive_row[0:1]
    pos_exp = jnp.exp(positive)
    total = pos_exp
    for k in range(sums.shape[0]):
        total = total + sums[k]
    loss[...] = jnp.log(total) - positive
    probs = (exps[...] / total).astype(BF16)
    part = dot(probs, user_bf[...]).astype(BF16)
    for k in range(item_part.shape[0]):
        item_part[k] = part[k * slots : (k + 1) * slots]
    all_cols[...] = to_columns([1.0 / total, pos_exp / total - 1.0])
    own_cols[...] = all_cols[pl.ds(pl.multiple_of(me[0] * share, share), share), :]


def final_kernel(item_recv, own_raw, own_cols, own_out, own_targets, *refs):
    user_parts, (d_user, d_samples) = refs[:-2], refs[-2:]
    slots = own_raw.shape[0]
    item_sum = item_recv[0].astype(F32)
    for k in range(1, item_recv.shape[0]):
        item_sum = item_sum + item_recv[k].astype(F32)
    own_unit, own_inv = unit_rows(own_raw[...])
    item_grad = INV_TEMP * item_sum
    d_samples[...] = own_inv * (
        item_grad - own_unit * jnp.sum(own_unit * item_grad, -1, keepdims=True)
    )
    user_unit, user_inv = unit_rows(own_out[...])
    target_unit, _ = unit_rows(own_targets[...].astype(F32))
    user_part = user_parts[0][...].astype(F32)
    for part in user_parts[1:]:
        user_part = user_part + part[...].astype(F32)
    user_grad = INV_TEMP * (user_part * own_cols[:, 0:1] + own_cols[:, 1:2] * target_unit)
    d_user[...] = user_inv * (
        user_grad - user_unit * jnp.sum(user_unit * user_grad, -1, keepdims=True)
    )


def call(kernel, outs, scalars, *args, remote=(), scratch=(), limit=VMEM_LIMIT):
    smem = pl.BlockSpec(memory_space=pltpu.SMEM)
    vmem = pl.BlockSpec(memory_space=pltpu.VMEM)
    anywhere = pl.BlockSpec(memory_space=pl.ANY)
    return pl.pallas_call(
        kernel,
        out_shape=[jax.ShapeDtypeStruct(s, t) for s, t in outs],
        in_specs=[smem] * len(scalars) + [anywhere] * len(remote) + [vmem] * len(args),
        out_specs=[vmem] * len(outs),
        scratch_shapes=list(scratch),
        compiler_params=pltpu.CompilerParams(vmem_limit_bytes=limit),
    )(*scalars, *remote, *args)


def per_device(events, in_proj, out_proj, lengths, targets, item_table, sample_ids, sample_counts):
    n, width = events.shape
    dh = out_proj.shape[1]
    heads = lax.axis_size("mp")
    groups = lax.axis_size("dp")
    slots = sample_ids.shape[0]
    scored = slots * groups
    share = n // heads
    me = lax.axis_index("mp")
    me_ref = me.astype(jnp.int32).reshape(1)

    blocks, own_raw, gated, rest = call(
        functools.partial(first_kernel, groups),
        [
            ((scored, width + 128), BF16),
            ((slots, width), F32),
            ((dh + dh // 2 + STAT_ROWS, n), BF16),
            ((dh + dh // 2, width), BF16),
        ],
        [],
        remote=[
            sample_ids,
            sample_counts,
            lengths,
            item_table,
            events,
            in_proj.reshape(width, -1),
            out_proj.reshape(dh, width),
        ],
        scratch=[
            pltpu.SMEM(sample_ids.shape, jnp.int32),
            pltpu.SMEM(sample_counts.shape, jnp.int32),
            pltpu.SMEM(lengths.shape, jnp.int32),
            pltpu.VMEM(item_table.shape, BF16),
            pltpu.VMEM((n, width), BF16),
            pltpu.VMEM((width, 4 * dh), BF16),
            pltpu.VMEM((dh, width), BF16),
            pltpu.SemaphoreType.DMA((7,)),
        ],
        limit=FIRST_LIMIT,
    )
    samples = lax.all_to_all(blocks, "dp", 0, 0, tiled=True)
    gated = lax.all_gather(gated, "mp", axis=0)
    rest = lax.all_gather(rest, "mp", axis=0)

    chips = heads // 2
    exps, sums, positive_row, user_bf, keep, give, own_out, own_targets = call(
        functools.partial(score_kernel, share),
        [
            ((scored, n), F32),
            ((heads, 1, n), F32),
            ((8, n), F32),
            ((n, width), BF16),
            ((chips, share, width), BF16),
            ((chips, share, width), BF16),
            ((share, width), F32),
            ((share, width), BF16),
        ],
        [me_ref],
        gated,
        rest,
        events,
        targets,
        samples,
        scratch=[pltpu.VMEM((n, width), F32)],
    )
    got = lax.ppermute(give, "mp", [(k, k ^ 1) for k in range(heads)])
    half = chips // 2
    own, other = call(
        halve_kernel, [((half, share, width), BF16)] * 2, [me_ref], keep, got
    )
    sums, other = lax.optimization_barrier((sums, other))
    got = lax.ppermute(other, "mp", [(k, (k + heads // 2) % heads) for k in range(heads)])
    sums = lax.all_to_all(sums, "mp", 0, 0, tiled=True)
    sums, got = lax.optimization_barrier((sums, got))
    loss, item_part, own_cols = call(
        functools.partial(grad_kernel, share),
        [((1, n), F32), ((groups, slots, width), BF16), ((share, 128), F32)],
        [me_ref],
        sums,
        positive_row,
        exps,
        user_bf,
        scratch=[pltpu.VMEM((n, 128), F32)],
    )
    item_recv = lax.all_to_all(item_part, "dp", 0, 0, tiled=True)
    pieces = list(call(add_kernel, [((share, width), BF16)] * half, [], own, got))
    pieces = pieces[:1] + [
        lax.ppermute(pieces[hop], "mp", [(k, (k + 2 * hop) % heads) for k in range(heads)])
        for hop in range(1, half)
    ]
    d_user, d_samples = call(
        final_kernel,
        [((share, width), F32), ((slots, width), F32)],
        [],
        item_recv,
        own_raw,
        own_cols,
        own_out,
        own_targets,
        *pieces,
    )
    return (loss.reshape(-1), d_user, d_samples)


def solution(mesh):
    placed = (
        P("dp", None),
        P(None, "mp", None),
        P("mp", None, None),
        P("dp", None),
        P("dp", None),
        P(("dp", "mp"), None),
        P(("dp", "mp")),
        P(("dp", "mp")),
    )
    return jax.shard_map(
        per_device,
        mesh=mesh,
        in_specs=placed,
        out_specs=(P("dp"), P(("dp", "mp"), None), P(("dp", "mp"), None)),
        check_vma=False,
    )
```

```python
import functools
import math

import jax
import jax.numpy as jnp
from jax import lax
from jax.experimental import pallas as pl
from jax.experimental.pallas import tpu as pltpu
from jax.sharding import PartitionSpec as P

MAXLEN = 256
INV_TEMP = 20.0
EPSILON = 1e-06
F32 = jnp.float32
BF16 = jnp.bfloat16
STAT_ROWS = 8
FIRST_LIMIT = 62 * 1024 * 1024
VMEM_LIMIT = 40 * 1024 * 1024


def dot(a, b, dims=((1,), (0,))):
    return lax.dot_general(a, b, (dims, ((), ())), preferred_element_type=F32)


def silu(x):
    return x / (1.0 + jnp.exp(-x))


def split3(x):
    hi = x.astype(BF16).astype(F32)
    mid = (x - hi).astype(BF16).astype(F32)
    return hi, mid, x - hi - mid


def unit_rows(values):
    inv_norm = lax.rsqrt(jnp.mean(values * values, -1, keepdims=True) + EPSILON) / math.sqrt(
        values.shape[-1]
    )
    return (values * inv_norm, inv_norm)


def to_columns(rows):
    n = rows[0].shape[1]
    at = lax.broadcasted_iota(jnp.int32, (128, n), 0)
    block = jnp.broadcast_to(rows[-1], (128, n))
    for k in range(len(rows) - 1):
        block = jnp.where(at == k, rows[k], block)
    return block.T


def first_kernel(
    copies, ids_hbm, counts_hbm, lengths_hbm, table_hbm, events_hbm, weight_hbm, out_hbm,
    blocks, own_raw, small, attended_out, gate_out,
    ids, counts, lengths, table, events, weight, out_proj, sem,
):
    slots = own_raw.shape[0]
    count, width = table.shape
    n = events.shape[0]
    dh = out_proj.shape[0]
    loads = []
    for k, (source, target) in enumerate(
        [
            (ids_hbm, ids),
            (counts_hbm, counts),
            (lengths_hbm, lengths),
            (table_hbm, table),
            (events_hbm, events),
            (weight_hbm, weight),
            (out_hbm, out_proj),
        ]
    ):
        loads.append(pltpu.make_async_copy(source, target, sem.at[k]))
        loads[-1].start()

    loads[0].wait()
    loads[1].wait()
    slot = lax.broadcasted_iota(jnp.int32, (slots, count), 0)
    at = lax.broadcasted_iota(jnp.int32, (slots, count), 1)
    wanted = jnp.zeros((slots, count), jnp.int32)
    drawn = jnp.ones((slots, 128), jnp.int32)
    slot_narrow = lax.broadcasted_iota(jnp.int32, (slots, 128), 0)
    for k in range(slots):
        wanted = jnp.where(slot == k, lax.rem(ids[k], count), wanted)
        drawn = jnp.where(slot_narrow == k, counts[k], drawn)
    logs = jnp.log(drawn.astype(F32))
    loads[3].wait()
    raw = dot((at == wanted).astype(F32).astype(BF16), table[...])
    own_raw[...] = raw
    unit, _ = unit_rows(raw)
    pack = jnp.concatenate([unit, logs], 1)
    twice = jnp.concatenate([pack, pack], 0).astype(BF16)
    for k in range(copies // 2):
        blocks[2 * k * slots : 2 * (k + 1) * slots, :] = twice

    loads[2].wait()
    position = lax.broadcasted_iota(jnp.int32, (1, n), 1)
    first = jnp.zeros((1, n), jnp.int32)
    end = jnp.int32(0)
    for k in range(lengths.shape[1]):
        end = end + lengths[0, k]
        first = jnp.where(position >= end, end, first)
    j_at = lax.broadcasted_iota(jnp.int32, (n, n), 0)
    seen = (j_at <= position) & (j_at >= first)
    loads[4].wait()
    wide = events[...].astype(F32)
    normed = (wide * lax.rsqrt(jnp.mean(wide * wide, -1, keepdims=True) + EPSILON)).astype(BF16)
    loads[5].wait()
    proj = silu(dot(normed, weight[...]))
    turned = proj.T
    gate = turned[:dh]
    value = turned[dh : 2 * dh].astype(BF16)
    query = turned[2 * dh : 3 * dh].astype(BF16)
    key = proj[:, 3 * dh :].astype(BF16)
    scores = dot(key, query)
    weights = (jnp.where(seen, silu(scores), 0.0) / MAXLEN).astype(BF16)
    attended = dot(value, weights)
    sums = split3(jnp.sum(attended, 0, keepdims=True))
    squares = split3(jnp.sum(attended * attended, 0, keepdims=True))
    at = lax.broadcasted_iota(jnp.int32, (STAT_ROWS, n), 0)
    loads[6].wait()
    last = out_proj[...].astype(F32)[dh - 1 :]
    rows = jnp.zeros((STAT_ROWS, n), F32)
    for k, row in enumerate(sums + squares + (last,)):
        rows = jnp.where(at == k, row, rows)
    rows = rows.astype(BF16)
    for k in range(small.shape[0]):
        small[k] = rows
    attended_out[...] = attended
    gate_out[...] = gate


def mix_kernel(small, attended, gate, out_proj, payload):
    heads = small.shape[0]
    dh = attended.shape[0]
    stats = small[0].astype(F32)
    for h in range(1, heads):
        stats = stats + small[h].astype(F32)
    full = heads * dh
    row_mean = (stats[0:1] + stats[1:2] + stats[2:3]) / full
    row_sq = (stats[3:4] + stats[4:5] + stats[5:6]) / full
    scale = lax.rsqrt(jnp.maximum(row_sq - row_mean * row_mean, 0.0) + EPSILON)
    payload[0:dh, :] = ((attended[...] - row_mean) * scale * gate[...]).astype(BF16)
    payload[dh:, :] = out_proj[0 : dh - 1, :]


def score_kernel(
    share, me, gathered, small, events, targets, samples,
    exps, sums, positive_row, user_bf, keep, give, own_out, own_targets, out_rows, chunks,
):
    n, width = events.shape
    heads = gathered.shape[0]
    dh = (gathered.shape[1] + 1) // 2
    mixed_in = jnp.concatenate([gathered[h, :dh, :] for h in range(heads)], 0)
    matrix = []
    for h in range(heads):
        matrix += [gathered[h, dh:, :].astype(F32), small[h].astype(F32)[6:7]]
    matrix = jnp.concatenate(matrix, 0).astype(BF16)
    mixed = dot(mixed_in, matrix, ((0,), (0,)))
    output = events[...].astype(F32) + mixed
    out_rows[...] = output
    own = pl.ds(pl.multiple_of(me[0] * share, share), share)
    own_out[...] = out_rows[own, :]
    own_targets[...] = targets[own, :]
    unit, _ = unit_rows(output)
    rounded = unit.astype(BF16)
    user_bf[...] = rounded
    target_unit, _ = unit_rows(targets[...].astype(F32))
    positive = INV_TEMP * jnp.sum(rounded.astype(F32) * target_unit, -1, keepdims=True)
    positive_row[...] = jnp.broadcast_to(positive, (n, 128)).T[0:8]
    sample_bf = samples[:, :width]
    log_counts = samples[:, width : width + 128].astype(F32)[:, 0:1]
    neg_exp = jnp.exp(INV_TEMP * dot(sample_bf, rounded, ((1,), (1,))) - log_counts)
    exps[...] = neg_exp
    user_part = dot(neg_exp.astype(BF16), sample_bf, ((0,), (0,))).astype(BF16)
    sums[...] = jnp.broadcast_to(jnp.sum(neg_exp, 0, keepdims=True)[None], sums.shape)
    chips, rows = chunks.shape[:2]
    half = chips // 2
    for z in range(chips):
        chunks[z] = user_part[z * rows : (z + 1) * rows]
    for hop in range(half):
        keep[hop] = chunks[lax.rem(me[0] // 2 + hop, chips)]
        give[hop] = chunks[lax.rem(me[0] // 2 + hop + half, chips)]


def grad_kernel(
    share, me, sums, positive_row, exps, user_bf, keep, got,
    loss, item_part, own_cols, mine, theirs, all_cols,
):
    slots = item_part.shape[1]
    positive = positive_row[0:1]
    pos_exp = jnp.exp(positive)
    total = pos_exp
    for k in range(sums.shape[0]):
        total = total + sums[k]
    loss[...] = jnp.log(total) - positive
    probs = (exps[...] / total).astype(BF16)
    part = dot(probs, user_bf[...]).astype(BF16)
    for k in range(item_part.shape[0]):
        item_part[k] = part[k * slots : (k + 1) * slots]
    all_cols[...] = to_columns([1.0 / total, pos_exp / total - 1.0])
    own_cols[...] = all_cols[pl.ds(pl.multiple_of(me[0] * share, share), share), :]
    first_core = lax.rem(me[0], 2) == 0
    for hop in range(keep.shape[0]):
        both = (keep[hop].astype(F32) + got[hop].astype(F32)).astype(BF16)
        mine[hop] = jnp.where(first_core, both[:share], both[share:])
        theirs[hop] = jnp.where(first_core, both[share:], both[:share])


def add_kernel(own, got, *pieces):
    for hop in range(len(pieces)):
        pieces[hop][...] = (own[hop].astype(F32) + got[hop].astype(F32)).astype(BF16)


def final_kernel(item_recv, own_raw, own_cols, own_out, own_targets, *refs):
    user_parts, (d_user, d_samples) = refs[:-2], refs[-2:]
    slots = own_raw.shape[0]
    item_sum = item_recv[0].astype(F32)
    for k in range(1, item_recv.shape[0]):
        item_sum = item_sum + item_recv[k].astype(F32)
    own_unit, own_inv = unit_rows(own_raw[...])
    item_grad = INV_TEMP * item_sum
    d_samples[...] = own_inv * (
        item_grad - own_unit * jnp.sum(own_unit * item_grad, -1, keepdims=True)
    )
    user_unit, user_inv = unit_rows(own_out[...])
    target_unit, _ = unit_rows(own_targets[...].astype(F32))
    user_part = user_parts[0][...].astype(F32)
    for part in user_parts[1:]:
        user_part = user_part + part[...].astype(F32)
    user_grad = INV_TEMP * (user_part * own_cols[:, 0:1] + own_cols[:, 1:2] * target_unit)
    d_user[...] = user_inv * (
        user_grad - user_unit * jnp.sum(user_unit * user_grad, -1, keepdims=True)
    )


def call(kernel, outs, scalars, *args, remote=(), scratch=(), limit=VMEM_LIMIT):
    smem = pl.BlockSpec(memory_space=pltpu.SMEM)
    vmem = pl.BlockSpec(memory_space=pltpu.VMEM)
    anywhere = pl.BlockSpec(memory_space=pl.ANY)
    return pl.pallas_call(
        kernel,
        out_shape=[jax.ShapeDtypeStruct(s, t) for s, t in outs],
        in_specs=[smem] * len(scalars) + [anywhere] * len(remote) + [vmem] * len(args),
        out_specs=[vmem] * len(outs),
        scratch_shapes=list(scratch),
        compiler_params=pltpu.CompilerParams(vmem_limit_bytes=limit),
    )(*scalars, *remote, *args)


def per_device(events, in_proj, out_proj, lengths, targets, item_table, sample_ids, sample_counts):
    n, width = events.shape
    dh = out_proj.shape[1]
    heads = lax.axis_size("mp")
    groups = lax.axis_size("dp")
    slots = sample_ids.shape[0]
    scored = slots * groups
    share = n // heads
    me = lax.axis_index("mp")
    me_ref = me.astype(jnp.int32).reshape(1)

    out_rows = out_proj.reshape(dh, width)
    blocks, own_raw, small, attended, gate = call(
        functools.partial(first_kernel, groups),
        [
            ((scored, width + 128), BF16),
            ((slots, width), F32),
            ((heads, STAT_ROWS, n), BF16),
            ((dh, n), F32),
            ((dh, n), F32),
        ],
        [],
        remote=[
            sample_ids,
            sample_counts,
            lengths,
            item_table,
            events,
            in_proj.reshape(width, -1),
            out_rows,
        ],
        scratch=[
            pltpu.SMEM(sample_ids.shape, jnp.int32),
            pltpu.SMEM(sample_counts.shape, jnp.int32),
            pltpu.SMEM(lengths.shape, jnp.int32),
            pltpu.VMEM(item_table.shape, BF16),
            pltpu.VMEM((n, width), BF16),
            pltpu.VMEM((width, 4 * dh), BF16),
            pltpu.VMEM((dh, width), BF16),
            pltpu.SemaphoreType.DMA((7,)),
        ],
        limit=FIRST_LIMIT,
    )
    small = lax.all_to_all(small, "mp", 0, 0, tiled=True)
    small, blocks = lax.optimization_barrier((small, blocks))
    samples = lax.all_to_all(blocks, "dp", 0, 0, tiled=True)
    (payload,) = call(
        mix_kernel, [((2 * dh - 1, n), BF16)], [], small, attended, gate, out_rows
    )
    gathered = lax.all_gather(payload, "mp", axis=0)

    chips = heads // 2
    half = chips // 2
    exps, sums, positive_row, user_bf, keep, give, own_out, own_targets = call(
        functools.partial(score_kernel, share),
        [
            ((scored, n), F32),
            ((heads, 1, n), F32),
            ((8, n), F32),
            ((n, width), BF16),
            ((half, 2 * share, width), BF16),
            ((half, 2 * share, width), BF16),
            ((share, width), F32),
            ((share, width), BF16),
        ],
        [me_ref],
        gathered,
        small,
        events,
        targets,
        samples,
        scratch=[pltpu.VMEM((n, width), F32), pltpu.VMEM((chips, 2 * share, width), BF16)],
    )
    got = lax.ppermute(give, "mp", [(k, (k + heads // 2) % heads) for k in range(heads)])
    sums = lax.all_to_all(sums, "mp", 0, 0, tiled=True)
    sums, got = lax.optimization_barrier((sums, got))
    loss, item_part, own_cols, mine, theirs = call(
        functools.partial(grad_kernel, share),
        [((1, n), F32), ((groups, slots, width), BF16), ((share, 128), F32)]
        + [((half, share, width), BF16)] * 2,
        [me_ref],
        sums,
        positive_row,
        exps,
        user_bf,
        keep,
        got,
        scratch=[pltpu.VMEM((n, 128), F32)],
    )
    item_recv = lax.all_to_all(item_part, "dp", 0, 0, tiled=True)
    got = lax.ppermute(theirs, "mp", [(k, k ^ 1) for k in range(heads)])
    pieces = list(call(add_kernel, [((share, width), BF16)] * half, [], mine, got))
    pieces = pieces[:1] + [
        lax.ppermute(pieces[hop], "mp", [(k, (k + 2 * hop) % heads) for k in range(heads)])
        for hop in range(1, half)
    ]
    d_user, d_samples = call(
        final_kernel,
        [((share, width), F32), ((slots, width), F32)],
        [],
        item_recv,
        own_raw,
        own_cols,
        own_out,
        own_targets,
        *pieces,
    )
    return (loss.reshape(-1), d_user, d_samples)


def solution(mesh):
    placed = (
        P("dp", None),
        P(None, "mp", None),
        P("mp", None, None),
        P("dp", None),
        P("dp", None),
        P(("dp", "mp"), None),
        P(("dp", "mp")),
        P(("dp", "mp")),
    )
    return jax.shard_map(
        per_device,
        mesh=mesh,
        in_specs=placed,
        out_specs=(P("dp"), P(("dp", "mp"), None), P(("dp", "mp"), None)),
        check_vma=False,
    )
```

```python
import functools
import math

import jax
import jax.numpy as jnp
from jax import lax
from jax.experimental import pallas as pl
from jax.experimental.pallas import tpu as pltpu
from jax.sharding import PartitionSpec as P

MAXLEN = 256
INV_TEMP = 20.0
EPSILON = 1e-06
F32 = jnp.float32
BF16 = jnp.bfloat16
STAT_ROWS = 8
FIRST_LIMIT = 62 * 1024 * 1024
VMEM_LIMIT = 40 * 1024 * 1024


def dot(a, b, dims=((1,), (0,))):
    return lax.dot_general(a, b, (dims, ((), ())), preferred_element_type=F32)


def silu(x):
    return x / (1.0 + jnp.exp(-x))


def split3(x):
    hi = x.astype(BF16).astype(F32)
    mid = (x - hi).astype(BF16).astype(F32)
    return hi, mid, x - hi - mid


def unit_rows(values):
    inv_norm = lax.rsqrt(jnp.mean(values * values, -1, keepdims=True) + EPSILON) / math.sqrt(
        values.shape[-1]
    )
    return (values * inv_norm, inv_norm)


def to_columns(rows):
    n = rows[0].shape[1]
    at = lax.broadcasted_iota(jnp.int32, (128, n), 0)
    block = jnp.broadcast_to(rows[-1], (128, n))
    for k in range(len(rows) - 1):
        block = jnp.where(at == k, rows[k], block)
    return block.T


def first_kernel(
    copies, ids_hbm, counts_hbm, lengths_hbm, table_hbm, events_hbm, weight_hbm, out_hbm,
    blocks, own_raw, small, attended_out, gate_out,
    ids, counts, lengths, table, events, weight, out_proj, sem,
):
    slots = own_raw.shape[0]
    count, width = table.shape
    n = events.shape[0]
    dh = out_proj.shape[0]
    loads = []
    for k, (source, target) in enumerate(
        [
            (ids_hbm, ids),
            (counts_hbm, counts),
            (lengths_hbm, lengths),
            (table_hbm, table),
            (events_hbm, events),
            (weight_hbm, weight),
            (out_hbm, out_proj),
        ]
    ):
        loads.append(pltpu.make_async_copy(source, target, sem.at[k]))
        loads[-1].start()

    loads[0].wait()
    loads[1].wait()
    slot = lax.broadcasted_iota(jnp.int32, (slots, count), 0)
    at = lax.broadcasted_iota(jnp.int32, (slots, count), 1)
    wanted = jnp.zeros((slots, count), jnp.int32)
    drawn = jnp.ones((slots, 128), jnp.int32)
    slot_narrow = lax.broadcasted_iota(jnp.int32, (slots, 128), 0)
    for k in range(slots):
        wanted = jnp.where(slot == k, lax.rem(ids[k], count), wanted)
        drawn = jnp.where(slot_narrow == k, counts[k], drawn)
    logs = jnp.log(drawn.astype(F32))
    loads[3].wait()
    raw = dot((at == wanted).astype(F32).astype(BF16), table[...])
    own_raw[...] = raw
    unit, _ = unit_rows(raw)
    pack = jnp.concatenate([unit, logs], 1)
    twice = jnp.concatenate([pack, pack], 0).astype(BF16)
    for k in range(copies // 2):
        blocks[2 * k * slots : 2 * (k + 1) * slots, :] = twice

    loads[2].wait()
    position = lax.broadcasted_iota(jnp.int32, (1, n), 1)
    first = jnp.zeros((1, n), jnp.int32)
    end = jnp.int32(0)
    for k in range(lengths.shape[1]):
        end = end + lengths[0, k]
        first = jnp.where(position >= end, end, first)
    j_at = lax.broadcasted_iota(jnp.int32, (n, n), 0)
    seen = (j_at <= position) & (j_at >= first)
    loads[4].wait()
    wide = events[...].astype(F32)
    normed = (wide * lax.rsqrt(jnp.mean(wide * wide, -1, keepdims=True) + EPSILON)).astype(BF16)
    loads[5].wait()
    proj = silu(dot(normed, weight[...]))
    turned = proj.T
    gate = turned[:dh]
    value = turned[dh : 2 * dh].astype(BF16)
    query = turned[2 * dh : 3 * dh].astype(BF16)
    key = proj[:, 3 * dh :].astype(BF16)
    scores = dot(key, query)
    weights = (jnp.where(seen, silu(scores), 0.0) / MAXLEN).astype(BF16)
    attended = dot(value, weights)
    sums = split3(jnp.sum(attended, 0, keepdims=True))
    squares = split3(jnp.sum(attended * attended, 0, keepdims=True))
    at = lax.broadcasted_iota(jnp.int32, (STAT_ROWS, n), 0)
    loads[6].wait()
    last = out_proj[...].astype(F32)[dh - 1 :]
    rows = jnp.zeros((STAT_ROWS, n), F32)
    for k, row in enumerate(sums + squares + (last,)):
        rows = jnp.where(at == k, row, rows)
    rows = rows.astype(BF16)
    for k in range(small.shape[0]):
        small[k] = rows
    attended_out[...] = attended
    gate_out[...] = gate


def mix_kernel(small, attended, gate, out_proj, payload):
    heads = small.shape[0]
    dh = attended.shape[0]
    stats = small[0].astype(F32)
    for h in range(1, heads):
        stats = stats + small[h].astype(F32)
    full = heads * dh
    row_mean = (stats[0:1] + stats[1:2] + stats[2:3]) / full
    row_sq = (stats[3:4] + stats[4:5] + stats[5:6]) / full
    scale = lax.rsqrt(jnp.maximum(row_sq - row_mean * row_mean, 0.0) + EPSILON)
    payload[0:dh, :] = ((attended[...] - row_mean) * scale * gate[...]).astype(BF16)
    payload[dh:, :] = out_proj[0 : dh - 1, :]


def score_kernel(
    share, me, gathered, small, events, targets, samples,
    exps, sums, positive_row, user_bf, keep, give, own_out, own_targets, out_rows, chunks,
):
    n, width = events.shape
    heads = gathered.shape[0]
    dh = (gathered.shape[1] + 1) // 2
    mixed_in = jnp.concatenate([gathered[h, :dh, :] for h in range(heads)], 0)
    matrix = []
    for h in range(heads):
        matrix += [gathered[h, dh:, :].astype(F32), small[h].astype(F32)[6:7]]
    matrix = jnp.concatenate(matrix, 0).astype(BF16)
    mixed = dot(mixed_in, matrix, ((0,), (0,)))
    output = events[...].astype(F32) + mixed
    out_rows[...] = output
    own = pl.ds(pl.multiple_of(me[0] * share, share), share)
    own_out[...] = out_rows[own, :]
    own_targets[...] = targets[own, :]
    unit, _ = unit_rows(output)
    rounded = unit.astype(BF16)
    user_bf[...] = rounded
    target_unit, _ = unit_rows(targets[...].astype(F32))
    positive = INV_TEMP * jnp.sum(rounded.astype(F32) * target_unit, -1, keepdims=True)
    positive_row[...] = jnp.broadcast_to(positive, (n, 128)).T[0:8]
    sample_bf = samples[:, :width]
    log_counts = samples[:, width : width + 128].astype(F32)[:, 0:1]
    neg_exp = jnp.exp(INV_TEMP * dot(sample_bf, rounded, ((1,), (1,))) - log_counts)
    exps[...] = neg_exp
    user_part = dot(neg_exp.astype(BF16), sample_bf, ((0,), (0,))).astype(BF16)
    sums[...] = jnp.broadcast_to(jnp.sum(neg_exp, 0, keepdims=True)[None], sums.shape)
    chips, rows = chunks.shape[:2]
    half = chips // 2
    for z in range(chips):
        chunks[z] = user_part[z * rows : (z + 1) * rows]
    chip = me[0] // 2
    neighbour = chip + 1 - 2 * lax.rem(chip, 2)
    for hop in range(half):
        keep[hop] = chunks[lax.rem(chip + 2 * hop, chips)]
        give[hop] = chunks[lax.rem(neighbour + 2 * hop, chips)]


def grad_kernel(
    share, me, sums, positive_row, exps, user_bf, keep, got,
    loss, item_part, own_cols, mine, theirs, all_cols,
):
    slots = item_part.shape[1]
    positive = positive_row[0:1]
    pos_exp = jnp.exp(positive)
    total = pos_exp
    for k in range(sums.shape[0]):
        total = total + sums[k]
    loss[...] = jnp.log(total) - positive
    probs = (exps[...] / total).astype(BF16)
    part = dot(probs, user_bf[...]).astype(BF16)
    for k in range(item_part.shape[0]):
        item_part[k] = part[k * slots : (k + 1) * slots]
    all_cols[...] = to_columns([1.0 / total, pos_exp / total - 1.0])
    own_cols[...] = all_cols[pl.ds(pl.multiple_of(me[0] * share, share), share), :]
    first_core = lax.rem(me[0], 2) == 0
    for hop in range(keep.shape[0]):
        both = (keep[hop].astype(F32) + got[hop].astype(F32)).astype(BF16)
        mine[hop] = jnp.where(first_core, both[:share], both[share:])
        theirs[hop] = jnp.where(first_core, both[share:], both[:share])


def add_kernel(own, got, *pieces):
    for hop in range(len(pieces)):
        pieces[hop][...] = (own[hop].astype(F32) + got[hop].astype(F32)).astype(BF16)


def final_kernel(item_recv, own_raw, own_cols, own_out, own_targets, *refs):
    user_parts, (d_user, d_samples) = refs[:-2], refs[-2:]
    slots = own_raw.shape[0]
    item_sum = item_recv[0].astype(F32)
    for k in range(1, item_recv.shape[0]):
        item_sum = item_sum + item_recv[k].astype(F32)
    own_unit, own_inv = unit_rows(own_raw[...])
    item_grad = INV_TEMP * item_sum
    d_samples[...] = own_inv * (
        item_grad - own_unit * jnp.sum(own_unit * item_grad, -1, keepdims=True)
    )
    user_unit, user_inv = unit_rows(own_out[...])
    target_unit, _ = unit_rows(own_targets[...].astype(F32))
    user_part = user_parts[0][...].astype(F32)
    for part in user_parts[1:]:
        user_part = user_part + part[...].astype(F32)
    user_grad = INV_TEMP * (user_part * own_cols[:, 0:1] + own_cols[:, 1:2] * target_unit)
    d_user[...] = user_inv * (
        user_grad - user_unit * jnp.sum(user_unit * user_grad, -1, keepdims=True)
    )


def call(kernel, outs, scalars, *args, remote=(), scratch=(), limit=VMEM_LIMIT):
    smem = pl.BlockSpec(memory_space=pltpu.SMEM)
    vmem = pl.BlockSpec(memory_space=pltpu.VMEM)
    anywhere = pl.BlockSpec(memory_space=pl.ANY)
    return pl.pallas_call(
        kernel,
        out_shape=[jax.ShapeDtypeStruct(s, t) for s, t in outs],
        in_specs=[smem] * len(scalars) + [anywhere] * len(remote) + [vmem] * len(args),
        out_specs=[vmem] * len(outs),
        scratch_shapes=list(scratch),
        compiler_params=pltpu.CompilerParams(vmem_limit_bytes=limit),
    )(*scalars, *remote, *args)


def per_device(events, in_proj, out_proj, lengths, targets, item_table, sample_ids, sample_counts):
    n, width = events.shape
    dh = out_proj.shape[1]
    heads = lax.axis_size("mp")
    groups = lax.axis_size("dp")
    slots = sample_ids.shape[0]
    scored = slots * groups
    share = n // heads
    me = lax.axis_index("mp")
    me_ref = me.astype(jnp.int32).reshape(1)

    out_rows = out_proj.reshape(dh, width)
    blocks, own_raw, small, attended, gate = call(
        functools.partial(first_kernel, groups),
        [
            ((scored, width + 128), BF16),
            ((slots, width), F32),
            ((heads, STAT_ROWS, n), BF16),
            ((dh, n), F32),
            ((dh, n), F32),
        ],
        [],
        remote=[
            sample_ids,
            sample_counts,
            lengths,
            item_table,
            events,
            in_proj.reshape(width, -1),
            out_rows,
        ],
        scratch=[
            pltpu.SMEM(sample_ids.shape, jnp.int32),
            pltpu.SMEM(sample_counts.shape, jnp.int32),
            pltpu.SMEM(lengths.shape, jnp.int32),
            pltpu.VMEM(item_table.shape, BF16),
            pltpu.VMEM((n, width), BF16),
            pltpu.VMEM((width, 4 * dh), BF16),
            pltpu.VMEM((dh, width), BF16),
            pltpu.SemaphoreType.DMA((7,)),
        ],
        limit=FIRST_LIMIT,
    )
    small = lax.all_to_all(small, "mp", 0, 0, tiled=True)
    small, blocks = lax.optimization_barrier((small, blocks))
    samples = lax.all_to_all(blocks, "dp", 0, 0, tiled=True)
    (payload,) = call(
        mix_kernel, [((2 * dh - 1, n), BF16)], [], small, attended, gate, out_rows
    )
    gathered = lax.all_gather(payload, "mp", axis=0)

    chips = heads // 2
    half = chips // 2
    exps, sums, positive_row, user_bf, keep, give, own_out, own_targets = call(
        functools.partial(score_kernel, share),
        [
            ((scored, n), F32),
            ((heads, 1, n), F32),
            ((8, n), F32),
            ((n, width), BF16),
            ((half, 2 * share, width), BF16),
            ((half, 2 * share, width), BF16),
            ((share, width), F32),
            ((share, width), BF16),
        ],
        [me_ref],
        gathered,
        small,
        events,
        targets,
        samples,
        scratch=[pltpu.VMEM((n, width), F32), pltpu.VMEM((chips, 2 * share, width), BF16)],
    )
    got = lax.ppermute(give, "mp", [(k, k ^ 2) for k in range(heads)])
    sums = lax.all_to_all(sums, "mp", 0, 0, tiled=True)
    sums, got = lax.optimization_barrier((sums, got))
    loss, item_part, own_cols, mine, theirs = call(
        functools.partial(grad_kernel, share),
        [((1, n), F32), ((groups, slots, width), BF16), ((share, 128), F32)]
        + [((half, share, width), BF16)] * 2,
        [me_ref],
        sums,
        positive_row,
        exps,
        user_bf,
        keep,
        got,
        scratch=[pltpu.VMEM((n, 128), F32)],
    )
    item_recv = lax.all_to_all(item_part, "dp", 0, 0, tiled=True)
    got = lax.ppermute(theirs, "mp", [(k, k ^ 1) for k in range(heads)])
    pieces = list(call(add_kernel, [((share, width), BF16)] * half, [], mine, got))
    pieces = pieces[:1] + [
        lax.ppermute(pieces[hop], "mp", [(k, (k + 4 * hop) % heads) for k in range(heads)])
        for hop in range(1, half)
    ]
    d_user, d_samples = call(
        final_kernel,
        [((share, width), F32), ((slots, width), F32)],
        [],
        item_recv,
        own_raw,
        own_cols,
        own_out,
        own_targets,
        *pieces,
    )
    return (loss.reshape(-1), d_user, d_samples)


def solution(mesh):
    placed = (
        P("dp", None),
        P(None, "mp", None),
        P("mp", None, None),
        P("dp", None),
        P("dp", None),
        P(("dp", "mp"), None),
        P(("dp", "mp")),
        P(("dp", "mp")),
    )
    return jax.shard_map(
        per_device,
        mesh=mesh,
        in_specs=placed,
        out_specs=(P("dp"), P(("dp", "mp"), None), P(("dp", "mp"), None)),
        check_vma=False,
    )
```

```python
import functools
import math

import jax
import jax.numpy as jnp
from jax import lax
from jax.experimental import pallas as pl
from jax.experimental.pallas import tpu as pltpu
from jax.sharding import PartitionSpec as P

MAXLEN = 256
INV_TEMP = 20.0
EPSILON = 1e-06
F32 = jnp.float32
BF16 = jnp.bfloat16
STAT_ROWS = 8
FIRST_LIMIT = 62 * 1024 * 1024
VMEM_LIMIT = 40 * 1024 * 1024


def dot(a, b, dims=((1,), (0,))):
    return lax.dot_general(a, b, (dims, ((), ())), preferred_element_type=F32)


def silu(x):
    return x / (1.0 + jnp.exp(-x))


def split3(x):
    hi = x.astype(BF16).astype(F32)
    mid = (x - hi).astype(BF16).astype(F32)
    return hi, mid, x - hi - mid


def unit_rows(values):
    inv_norm = lax.rsqrt(jnp.mean(values * values, -1, keepdims=True) + EPSILON) / math.sqrt(
        values.shape[-1]
    )
    return (values * inv_norm, inv_norm)


def to_columns(rows):
    n = rows[0].shape[1]
    at = lax.broadcasted_iota(jnp.int32, (128, n), 0)
    block = jnp.broadcast_to(rows[-1], (128, n))
    for k in range(len(rows) - 1):
        block = jnp.where(at == k, rows[k], block)
    return block.T


def first_kernel(
    copies, ids_hbm, counts_hbm, lengths_hbm, table_hbm, events_hbm, weight_hbm, out_hbm,
    blocks, own_raw, small, attended_out, gate_out,
    ids, counts, lengths, table, events, weight, out_proj, sem,
):
    slots = own_raw.shape[0]
    count, width = table.shape
    n = events.shape[0]
    dh = out_proj.shape[0]
    loads = []
    for k, (source, target) in enumerate(
        [
            (ids_hbm, ids),
            (counts_hbm, counts),
            (lengths_hbm, lengths),
            (table_hbm, table),
            (events_hbm, events),
            (weight_hbm, weight),
            (out_hbm, out_proj),
        ]
    ):
        loads.append(pltpu.make_async_copy(source, target, sem.at[k]))
        loads[-1].start()

    loads[0].wait()
    loads[1].wait()
    slot = lax.broadcasted_iota(jnp.int32, (slots, count), 0)
    at = lax.broadcasted_iota(jnp.int32, (slots, count), 1)
    wanted = jnp.zeros((slots, count), jnp.int32)
    drawn = jnp.ones((slots, 128), jnp.int32)
    slot_narrow = lax.broadcasted_iota(jnp.int32, (slots, 128), 0)
    for k in range(slots):
        wanted = jnp.where(slot == k, lax.rem(ids[k], count), wanted)
        drawn = jnp.where(slot_narrow == k, counts[k], drawn)
    logs = jnp.log(drawn.astype(F32))
    loads[3].wait()
    raw = dot((at == wanted).astype(F32).astype(BF16), table[...])
    own_raw[...] = raw
    unit, _ = unit_rows(raw)
    pack = jnp.concatenate([unit, logs], 1)
    twice = jnp.concatenate([pack, pack], 0).astype(BF16)
    for k in range(copies // 2):
        blocks[2 * k * slots : 2 * (k + 1) * slots, :] = twice

    loads[2].wait()
    position = lax.broadcasted_iota(jnp.int32, (1, n), 1)
    first = jnp.zeros((1, n), jnp.int32)
    end = jnp.int32(0)
    for k in range(lengths.shape[1]):
        end = end + lengths[0, k]
        first = jnp.where(position >= end, end, first)
    j_at = lax.broadcasted_iota(jnp.int32, (n, n), 0)
    seen = (j_at <= position) & (j_at >= first)
    loads[4].wait()
    wide = events[...].astype(F32)
    normed = (wide * lax.rsqrt(jnp.mean(wide * wide, -1, keepdims=True) + EPSILON)).astype(BF16)
    loads[5].wait()
    proj = silu(dot(normed, weight[...]))
    turned = proj.T
    gate = turned[:dh]
    value = turned[dh : 2 * dh].astype(BF16)
    query = turned[2 * dh : 3 * dh].astype(BF16)
    key = proj[:, 3 * dh :].astype(BF16)
    scores = dot(key, query)
    weights = (jnp.where(seen, silu(scores), 0.0) / MAXLEN).astype(BF16)
    attended = dot(value, weights)
    sums = split3(jnp.sum(attended, 0, keepdims=True))
    squares = split3(jnp.sum(attended * attended, 0, keepdims=True))
    at = lax.broadcasted_iota(jnp.int32, (STAT_ROWS, n), 0)
    loads[6].wait()
    last = out_proj[...].astype(F32)[dh - 1 :]
    rows = jnp.zeros((STAT_ROWS, n), F32)
    for k, row in enumerate(sums + squares + (last,)):
        rows = jnp.where(at == k, row, rows)
    rows = rows.astype(BF16)
    for k in range(small.shape[0]):
        small[k] = rows
    attended_out[...] = attended
    gate_out[...] = gate


def mix_kernel(small, attended, gate, out_proj, payload):
    heads = small.shape[0]
    dh = attended.shape[0]
    stats = small[0].astype(F32)
    for h in range(1, heads):
        stats = stats + small[h].astype(F32)
    full = heads * dh
    row_mean = (stats[0:1] + stats[1:2] + stats[2:3]) / full
    row_sq = (stats[3:4] + stats[4:5] + stats[5:6]) / full
    scale = lax.rsqrt(jnp.maximum(row_sq - row_mean * row_mean, 0.0) + EPSILON)
    payload[0:dh, :] = ((attended[...] - row_mean) * scale * gate[...]).astype(BF16)
    payload[dh:, :] = out_proj[0 : dh - 1, :]


def user_kernel(
    share, me, gathered, small, events, targets,
    positive_row, user_bf, own_out, own_targets, out_rows,
):
    n, width = events.shape
    heads = gathered.shape[0]
    dh = (gathered.shape[1] + 1) // 2
    mixed_in = jnp.concatenate([gathered[h, :dh, :] for h in range(heads)], 0)
    matrix = []
    for h in range(heads):
        matrix += [gathered[h, dh:, :].astype(F32), small[h].astype(F32)[6:7]]
    matrix = jnp.concatenate(matrix, 0).astype(BF16)
    output = events[...].astype(F32) + dot(mixed_in, matrix, ((0,), (0,)))
    out_rows[...] = output
    own = pl.ds(pl.multiple_of(me[0] * share, share), share)
    own_out[...] = out_rows[own, :]
    own_targets[...] = targets[own, :]
    unit, _ = unit_rows(output)
    rounded = unit.astype(BF16)
    user_bf[...] = rounded
    target_unit, _ = unit_rows(targets[...].astype(F32))
    positive = INV_TEMP * jnp.sum(rounded.astype(F32) * target_unit, -1, keepdims=True)
    positive_row[...] = jnp.broadcast_to(positive, (n, 128)).T[0:8]


def neighbours(chips):
    pairs = []
    for k in range(2 * chips):
        z, core = k // 2, k % 2
        step = 1 if z % 2 == core else -1
        pairs.append((k, 2 * ((z + step) % chips) + core))
    return pairs


def score_kernel(me, samples, user_bf, exps, sums, keep, give, chunks):
    width = user_bf.shape[1]
    sample_bf = samples[:, :width]
    log_counts = samples[:, width : width + 128].astype(F32)[:, 0:1]
    neg_exp = jnp.exp(INV_TEMP * dot(sample_bf, user_bf[...], ((1,), (1,))) - log_counts)
    exps[...] = neg_exp
    user_part = dot(neg_exp.astype(BF16), sample_bf, ((0,), (0,))).astype(BF16)
    sums[...] = jnp.broadcast_to(jnp.sum(neg_exp, 0, keepdims=True)[None], sums.shape)
    chips, rows = chunks.shape[:2]
    for z in range(chips):
        chunks[z] = user_part[z * rows : (z + 1) * rows]
    chip, core = me[0] // 2, lax.rem(me[0], 2)
    step = jnp.where(lax.rem(chip, 2) == core, 1, chips - 1)
    for hop in range(chips // 2):
        keep[hop] = chunks[lax.rem(chip + 2 * hop, chips)]
        give[hop] = chunks[lax.rem(chip + step + 2 * hop, chips)]


def grad_kernel(
    share, me, sums, positive_row, exps, user_bf, keep, got,
    loss, item_part, own_cols, mine, theirs, all_cols,
):
    slots = item_part.shape[1]
    positive = positive_row[0:1]
    pos_exp = jnp.exp(positive)
    total = pos_exp
    for k in range(sums.shape[0]):
        total = total + sums[k]
    loss[...] = jnp.log(total) - positive
    probs = (exps[...] / total).astype(BF16)
    part = dot(probs, user_bf[...]).astype(BF16)
    for k in range(item_part.shape[0]):
        item_part[k] = part[k * slots : (k + 1) * slots]
    all_cols[...] = to_columns([1.0 / total, pos_exp / total - 1.0])
    own_cols[...] = all_cols[pl.ds(pl.multiple_of(me[0] * share, share), share), :]
    first_core = lax.rem(me[0], 2) == 0
    for hop in range(keep.shape[0]):
        both = (keep[hop].astype(F32) + got[hop].astype(F32)).astype(BF16)
        mine[hop] = jnp.where(first_core, both[:share], both[share:])
        theirs[hop] = jnp.where(first_core, both[share:], both[:share])


def add_kernel(me, own, both, *pieces):
    other = 1 - lax.rem(me[0], 2)
    for hop in range(len(pieces)):
        pieces[hop][...] = (own[hop].astype(F32) + both[other, hop].astype(F32)).astype(BF16)


def final_kernel(item_recv, own_raw, own_cols, own_out, own_targets, *refs):
    user_parts, (d_user, d_samples) = refs[:-2], refs[-2:]
    slots = own_raw.shape[0]
    item_sum = item_recv[0].astype(F32)
    for k in range(1, item_recv.shape[0]):
        item_sum = item_sum + item_recv[k].astype(F32)
    own_unit, own_inv = unit_rows(own_raw[...])
    item_grad = INV_TEMP * item_sum
    d_samples[...] = own_inv * (
        item_grad - own_unit * jnp.sum(own_unit * item_grad, -1, keepdims=True)
    )
    user_unit, user_inv = unit_rows(own_out[...])
    target_unit, _ = unit_rows(own_targets[...].astype(F32))
    user_part = user_parts[0][...].astype(F32)
    for part in user_parts[1:]:
        user_part = user_part + part[...].astype(F32)
    user_grad = INV_TEMP * (user_part * own_cols[:, 0:1] + own_cols[:, 1:2] * target_unit)
    d_user[...] = user_inv * (
        user_grad - user_unit * jnp.sum(user_unit * user_grad, -1, keepdims=True)
    )


def call(kernel, outs, scalars, *args, remote=(), scratch=(), limit=VMEM_LIMIT):
    smem = pl.BlockSpec(memory_space=pltpu.SMEM)
    vmem = pl.BlockSpec(memory_space=pltpu.VMEM)
    anywhere = pl.BlockSpec(memory_space=pl.ANY)
    return pl.pallas_call(
        kernel,
        out_shape=[jax.ShapeDtypeStruct(s, t) for s, t in outs],
        in_specs=[smem] * len(scalars) + [anywhere] * len(remote) + [vmem] * len(args),
        out_specs=[vmem] * len(outs),
        scratch_shapes=list(scratch),
        compiler_params=pltpu.CompilerParams(vmem_limit_bytes=limit),
    )(*scalars, *remote, *args)


def per_device(events, in_proj, out_proj, lengths, targets, item_table, sample_ids, sample_counts):
    n, width = events.shape
    dh = out_proj.shape[1]
    heads = lax.axis_size("mp")
    groups = lax.axis_size("dp")
    slots = sample_ids.shape[0]
    scored = slots * groups
    share = n // heads
    me = lax.axis_index("mp")
    me_ref = me.astype(jnp.int32).reshape(1)

    out_rows = out_proj.reshape(dh, width)
    blocks, own_raw, small, attended, gate = call(
        functools.partial(first_kernel, groups),
        [
            ((scored, width + 128), BF16),
            ((slots, width), F32),
            ((heads, STAT_ROWS, n), BF16),
            ((dh, n), F32),
            ((dh, n), F32),
        ],
        [],
        remote=[
            sample_ids,
            sample_counts,
            lengths,
            item_table,
            events,
            in_proj.reshape(width, -1),
            out_rows,
        ],
        scratch=[
            pltpu.SMEM(sample_ids.shape, jnp.int32),
            pltpu.SMEM(sample_counts.shape, jnp.int32),
            pltpu.SMEM(lengths.shape, jnp.int32),
            pltpu.VMEM(item_table.shape, BF16),
            pltpu.VMEM((n, width), BF16),
            pltpu.VMEM((width, 4 * dh), BF16),
            pltpu.VMEM((dh, width), BF16),
            pltpu.SemaphoreType.DMA((7,)),
        ],
        limit=FIRST_LIMIT,
    )
    small = lax.all_to_all(small, "mp", 0, 0, tiled=True)
    small, blocks = lax.optimization_barrier((small, blocks))
    samples = lax.all_to_all(blocks, "dp", 0, 0, tiled=True)
    (payload,) = call(
        mix_kernel, [((2 * dh - 1, n), BF16)], [], small, attended, gate, out_rows
    )
    gathered = lax.all_gather(payload, "mp", axis=0)

    chips = heads // 2
    half = chips // 2
    positive_row, user_bf, own_out, own_targets = call(
        functools.partial(user_kernel, share),
        [((8, n), F32), ((n, width), BF16), ((share, width), F32), ((share, width), BF16)],
        [me_ref],
        gathered,
        small,
        events,
        targets,
        scratch=[pltpu.VMEM((n, width), F32)],
    )
    exps, sums, keep, give = call(
        score_kernel,
        [((scored, n), F32), ((heads, 1, n), F32)] + [((half, 2 * share, width), BF16)] * 2,
        [me_ref],
        samples,
        user_bf,
        scratch=[pltpu.VMEM((chips, 2 * share, width), BF16)],
    )
    got = lax.ppermute(give, "mp", neighbours(chips))
    sums = lax.all_to_all(sums, "mp", 0, 0, tiled=True)
    sums, got = lax.optimization_barrier((sums, got))
    loss, item_part, own_cols, mine, theirs = call(
        functools.partial(grad_kernel, share),
        [((1, n), F32), ((groups, slots, width), BF16), ((share, 128), F32)]
        + [((half, share, width), BF16)] * 2,
        [me_ref],
        sums,
        positive_row,
        exps,
        user_bf,
        keep,
        got,
        scratch=[pltpu.VMEM((n, 128), F32)],
    )
    item_recv = lax.all_to_all(item_part, "dp", 0, 0, tiled=True)
    cores = [[2 * z, 2 * z + 1] for z in range(chips)]
    both = lax.all_gather(theirs, "mp", axis=0, axis_index_groups=cores)
    pieces = list(call(add_kernel, [((share, width), BF16)] * half, [me_ref], mine, both))
    pieces = pieces[:1] + [
        lax.ppermute(pieces[hop], "mp", [(k, (k + 4 * hop) % heads) for k in range(heads)])
        for hop in range(1, half)
    ]
    d_user, d_samples = call(
        final_kernel,
        [((share, width), F32), ((slots, width), F32)],
        [],
        item_recv,
        own_raw,
        own_cols,
        own_out,
        own_targets,
        *pieces,
    )
    return (loss.reshape(-1), d_user, d_samples)


def solution(mesh):
    placed = (
        P("dp", None),
        P(None, "mp", None),
        P("mp", None, None),
        P("dp", None),
        P("dp", None),
        P(("dp", "mp"), None),
        P(("dp", "mp")),
        P(("dp", "mp")),
    )
    return jax.shard_map(
        per_device,
        mesh=mesh,
        in_specs=placed,
        out_specs=(P("dp"), P(("dp", "mp"), None), P(("dp", "mp"), None)),
        check_vma=False,
    )
```

```python
import functools
import math

import jax
import jax.numpy as jnp
from jax import lax
from jax.experimental import pallas as pl
from jax.experimental.pallas import tpu as pltpu
from jax.sharding import PartitionSpec as P

MAXLEN = 256
INV_TEMP = 20.0
EPSILON = 1e-06
F32 = jnp.float32
BF16 = jnp.bfloat16
STAT_ROWS = 8
FIRST_LIMIT = 62 * 1024 * 1024
VMEM_LIMIT = 40 * 1024 * 1024


def dot(a, b, dims=((1,), (0,))):
    return lax.dot_general(a, b, (dims, ((), ())), preferred_element_type=F32)


def silu(x):
    return x / (1.0 + jnp.exp(-x))


def split3(x):
    hi = x.astype(BF16).astype(F32)
    mid = (x - hi).astype(BF16).astype(F32)
    return hi, mid, x - hi - mid


def unit_rows(values):
    inv_norm = lax.rsqrt(jnp.mean(values * values, -1, keepdims=True) + EPSILON) / math.sqrt(
        values.shape[-1]
    )
    return (values * inv_norm, inv_norm)


def to_columns(rows):
    n = rows[0].shape[1]
    at = lax.broadcasted_iota(jnp.int32, (128, n), 0)
    block = jnp.broadcast_to(rows[-1], (128, n))
    for k in range(len(rows) - 1):
        block = jnp.where(at == k, rows[k], block)
    return block.T


def first_kernel(
    copies, ids_hbm, counts_hbm, lengths_hbm, table_hbm, events_hbm, weight_hbm, out_hbm,
    blocks, own_raw, small, attended_out, gate_out,
    ids, counts, lengths, table, events, weight, out_proj, sem,
):
    slots = own_raw.shape[0]
    count, width = table.shape
    n = events.shape[0]
    dh = out_proj.shape[0]
    loads = []
    for k, (source, target) in enumerate(
        [
            (ids_hbm, ids),
            (counts_hbm, counts),
            (lengths_hbm, lengths),
            (table_hbm, table),
            (events_hbm, events),
            (weight_hbm, weight),
            (out_hbm, out_proj),
        ]
    ):
        loads.append(pltpu.make_async_copy(source, target, sem.at[k]))
        loads[-1].start()

    loads[0].wait()
    loads[1].wait()
    slot = lax.broadcasted_iota(jnp.int32, (slots, count), 0)
    at = lax.broadcasted_iota(jnp.int32, (slots, count), 1)
    wanted = jnp.zeros((slots, count), jnp.int32)
    drawn = jnp.ones((slots, 128), jnp.int32)
    slot_narrow = lax.broadcasted_iota(jnp.int32, (slots, 128), 0)
    for k in range(slots):
        wanted = jnp.where(slot == k, lax.rem(ids[k], count), wanted)
        drawn = jnp.where(slot_narrow == k, counts[k], drawn)
    logs = jnp.log(drawn.astype(F32))
    loads[3].wait()
    raw = dot((at == wanted).astype(F32).astype(BF16), table[...])
    own_raw[...] = raw
    unit, _ = unit_rows(raw)
    pack = jnp.concatenate([unit, logs], 1)
    twice = jnp.concatenate([pack, pack], 0).astype(BF16)
    for k in range(copies // 2):
        blocks[2 * k * slots : 2 * (k + 1) * slots, :] = twice

    loads[2].wait()
    position = lax.broadcasted_iota(jnp.int32, (1, n), 1)
    first = jnp.zeros((1, n), jnp.int32)
    end = jnp.int32(0)
    for k in range(lengths.shape[1]):
        end = end + lengths[0, k]
        first = jnp.where(position >= end, end, first)
    j_at = lax.broadcasted_iota(jnp.int32, (n, n), 0)
    seen = (j_at <= position) & (j_at >= first)
    loads[4].wait()
    wide = events[...].astype(F32)
    normed = (wide * lax.rsqrt(jnp.mean(wide * wide, -1, keepdims=True) + EPSILON)).astype(BF16)
    loads[5].wait()
    proj = silu(dot(normed, weight[...]))
    turned = proj.T
    gate = turned[:dh]
    value = turned[dh : 2 * dh].astype(BF16)
    query = turned[2 * dh : 3 * dh].astype(BF16)
    key = proj[:, 3 * dh :].astype(BF16)
    scores = dot(key, query)
    weights = (jnp.where(seen, silu(scores), 0.0) / MAXLEN).astype(BF16)
    attended = dot(value, weights)
    sums = split3(jnp.sum(attended, 0, keepdims=True))
    squares = split3(jnp.sum(attended * attended, 0, keepdims=True))
    at = lax.broadcasted_iota(jnp.int32, (STAT_ROWS, n), 0)
    loads[6].wait()
    last = out_proj[...].astype(F32)[dh - 1 :]
    rows = jnp.zeros((STAT_ROWS, n), F32)
    for k, row in enumerate(sums + squares + (last,)):
        rows = jnp.where(at == k, row, rows)
    rows = rows.astype(BF16)
    for k in range(small.shape[0]):
        small[k] = rows
    attended_out[...] = attended
    gate_out[...] = gate


def mix_kernel(small, attended, gate, out_proj, payload):
    heads = small.shape[0]
    dh = attended.shape[0]
    stats = small[0].astype(F32)
    for h in range(1, heads):
        stats = stats + small[h].astype(F32)
    full = heads * dh
    row_mean = (stats[0:1] + stats[1:2] + stats[2:3]) / full
    row_sq = (stats[3:4] + stats[4:5] + stats[5:6]) / full
    scale = lax.rsqrt(jnp.maximum(row_sq - row_mean * row_mean, 0.0) + EPSILON)
    payload[0:dh, :] = ((attended[...] - row_mean) * scale * gate[...]).astype(BF16)
    payload[dh:, :] = out_proj[0 : dh - 1, :]


def user_kernel(
    share, me, gathered, small, events, targets,
    positive_row, user_bf, own_out, own_targets, out_rows,
):
    n, width = events.shape
    heads = gathered.shape[0]
    dh = (gathered.shape[1] + 1) // 2
    mixed_in = jnp.concatenate([gathered[h, :dh, :] for h in range(heads)], 0)
    matrix = []
    for h in range(heads):
        matrix += [gathered[h, dh:, :].astype(F32), small[h].astype(F32)[6:7]]
    matrix = jnp.concatenate(matrix, 0).astype(BF16)
    output = events[...].astype(F32) + dot(mixed_in, matrix, ((0,), (0,)))
    out_rows[...] = output
    own = pl.ds(pl.multiple_of(me[0] * share, share), share)
    own_out[...] = out_rows[own, :]
    own_targets[...] = targets[own, :]
    unit, _ = unit_rows(output)
    rounded = unit.astype(BF16)
    user_bf[...] = rounded
    target_unit, _ = unit_rows(targets[...].astype(F32))
    positive = INV_TEMP * jnp.sum(rounded.astype(F32) * target_unit, -1, keepdims=True)
    positive_row[...] = jnp.broadcast_to(positive, (n, 128)).T[0:8]


def neighbours(chips):
    pairs = []
    for k in range(2 * chips):
        z, core = k // 2, k % 2
        step = 1 if z % 2 == core else -1
        pairs.append((k, 2 * ((z + step) % chips) + core))
    return pairs


def score_kernel(me, samples, user_bf, exps, sums, keep, give, chunks):
    width = user_bf.shape[1]
    sample_bf = samples[:, :width]
    log_counts = samples[:, width : width + 128].astype(F32)[:, 0:1]
    neg_exp = jnp.exp(INV_TEMP * dot(sample_bf, user_bf[...], ((1,), (1,))) - log_counts)
    exps[...] = neg_exp
    user_part = dot(neg_exp.astype(BF16), sample_bf, ((0,), (0,))).astype(BF16)
    sums[...] = jnp.broadcast_to(jnp.sum(neg_exp, 0, keepdims=True)[None], sums.shape)
    chips, rows = chunks.shape[:2]
    for z in range(chips):
        chunks[z] = user_part[z * rows : (z + 1) * rows]
    chip, core = me[0] // 2, lax.rem(me[0], 2)
    step = jnp.where(lax.rem(chip, 2) == core, 1, chips - 1)
    for hop in range(chips // 2):
        keep[hop] = chunks[lax.rem(chip + 2 * hop, chips)]
        give[hop] = chunks[lax.rem(chip + step + 2 * hop, chips)]


def item_kernel(sums, positive_row, exps, user_bf, item_part, totals):
    slots = item_part.shape[1]
    total = jnp.exp(positive_row[0:1])
    for k in range(sums.shape[0]):
        total = total + sums[k]
    totals[...] = jnp.broadcast_to(total, totals.shape)
    probs = (exps[...] / total).astype(BF16)
    part = dot(probs, user_bf[...]).astype(BF16)
    for k in range(item_part.shape[0]):
        item_part[k] = part[k * slots : (k + 1) * slots]


def loss_kernel(share, me, totals, positive_row, keep, got, loss, own_cols, mine, theirs, all_cols):
    positive = positive_row[0:1]
    total = totals[0:1]
    loss[...] = jnp.log(total) - positive
    all_cols[...] = to_columns([1.0 / total, jnp.exp(positive) / total - 1.0])
    own_cols[...] = all_cols[pl.ds(pl.multiple_of(me[0] * share, share), share), :]
    first_core = lax.rem(me[0], 2) == 0
    for hop in range(keep.shape[0]):
        both = (keep[hop].astype(F32) + got[hop].astype(F32)).astype(BF16)
        mine[hop] = jnp.where(first_core, both[:share], both[share:])
        theirs[hop] = jnp.where(first_core, both[share:], both[:share])


def add_kernel(me, own, both, *pieces):
    other = 1 - lax.rem(me[0], 2)
    for hop in range(len(pieces)):
        pieces[hop][...] = (own[hop].astype(F32) + both[other, hop].astype(F32)).astype(BF16)


def user_grad_kernel(own_cols, own_out, own_targets, *refs):
    user_parts, d_user = refs[:-1], refs[-1]
    user_unit, user_inv = unit_rows(own_out[...])
    target_unit, _ = unit_rows(own_targets[...].astype(F32))
    user_part = user_parts[0][...].astype(F32)
    for part in user_parts[1:]:
        user_part = user_part + part[...].astype(F32)
    user_grad = INV_TEMP * (user_part * own_cols[:, 0:1] + own_cols[:, 1:2] * target_unit)
    d_user[...] = user_inv * (
        user_grad - user_unit * jnp.sum(user_unit * user_grad, -1, keepdims=True)
    )


def sample_grad_kernel(item_recv, own_raw, d_samples):
    own_unit, own_inv = unit_rows(own_raw[...])
    item_sum = item_recv[0].astype(F32)
    for k in range(1, item_recv.shape[0]):
        item_sum = item_sum + item_recv[k].astype(F32)
    item_grad = INV_TEMP * item_sum
    d_samples[...] = own_inv * (
        item_grad - own_unit * jnp.sum(own_unit * item_grad, -1, keepdims=True)
    )


def call(kernel, outs, scalars, *args, remote=(), scratch=(), limit=VMEM_LIMIT):
    smem = pl.BlockSpec(memory_space=pltpu.SMEM)
    vmem = pl.BlockSpec(memory_space=pltpu.VMEM)
    anywhere = pl.BlockSpec(memory_space=pl.ANY)
    return pl.pallas_call(
        kernel,
        out_shape=[jax.ShapeDtypeStruct(s, t) for s, t in outs],
        in_specs=[smem] * len(scalars) + [anywhere] * len(remote) + [vmem] * len(args),
        out_specs=[vmem] * len(outs),
        scratch_shapes=list(scratch),
        compiler_params=pltpu.CompilerParams(vmem_limit_bytes=limit),
    )(*scalars, *remote, *args)


def per_device(events, in_proj, out_proj, lengths, targets, item_table, sample_ids, sample_counts):
    n, width = events.shape
    dh = out_proj.shape[1]
    heads = lax.axis_size("mp")
    groups = lax.axis_size("dp")
    slots = sample_ids.shape[0]
    scored = slots * groups
    share = n // heads
    me = lax.axis_index("mp")
    me_ref = me.astype(jnp.int32).reshape(1)

    out_rows = out_proj.reshape(dh, width)
    blocks, own_raw, small, attended, gate = call(
        functools.partial(first_kernel, groups),
        [
            ((scored, width + 128), BF16),
            ((slots, width), F32),
            ((heads, STAT_ROWS, n), BF16),
            ((dh, n), F32),
            ((dh, n), F32),
        ],
        [],
        remote=[
            sample_ids,
            sample_counts,
            lengths,
            item_table,
            events,
            in_proj.reshape(width, -1),
            out_rows,
        ],
        scratch=[
            pltpu.SMEM(sample_ids.shape, jnp.int32),
            pltpu.SMEM(sample_counts.shape, jnp.int32),
            pltpu.SMEM(lengths.shape, jnp.int32),
            pltpu.VMEM(item_table.shape, BF16),
            pltpu.VMEM((n, width), BF16),
            pltpu.VMEM((width, 4 * dh), BF16),
            pltpu.VMEM((dh, width), BF16),
            pltpu.SemaphoreType.DMA((7,)),
        ],
        limit=FIRST_LIMIT,
    )
    small = lax.all_to_all(small, "mp", 0, 0, tiled=True)
    small, blocks = lax.optimization_barrier((small, blocks))
    samples = lax.all_to_all(blocks, "dp", 0, 0, tiled=True)
    (payload,) = call(
        mix_kernel, [((2 * dh - 1, n), BF16)], [], small, attended, gate, out_rows
    )
    gathered = lax.all_gather(payload, "mp", axis=0)

    chips = heads // 2
    half = chips // 2
    positive_row, user_bf, own_out, own_targets = call(
        functools.partial(user_kernel, share),
        [((8, n), F32), ((n, width), BF16), ((share, width), F32), ((share, width), BF16)],
        [me_ref],
        gathered,
        small,
        events,
        targets,
        scratch=[pltpu.VMEM((n, width), F32)],
    )
    exps, sums, keep, give = call(
        score_kernel,
        [((scored, n), F32), ((heads, 1, n), F32)] + [((half, 2 * share, width), BF16)] * 2,
        [me_ref],
        samples,
        user_bf,
        scratch=[pltpu.VMEM((chips, 2 * share, width), BF16)],
    )
    got = lax.ppermute(give, "mp", neighbours(chips))
    sums = lax.all_to_all(sums, "mp", 0, 0, tiled=True)
    sums, got = lax.optimization_barrier((sums, got))
    item_part, totals = call(
        item_kernel,
        [((groups, slots, width), BF16), ((8, n), F32)],
        [],
        sums,
        positive_row,
        exps,
        user_bf,
    )
    item_recv = lax.all_to_all(item_part, "dp", 0, 0, tiled=True)
    loss, own_cols, mine, theirs = call(
        functools.partial(loss_kernel, share),
        [((1, n), F32), ((share, 128), F32)] + [((half, share, width), BF16)] * 2,
        [me_ref],
        totals,
        positive_row,
        keep,
        got,
        scratch=[pltpu.VMEM((n, 128), F32)],
    )
    cores = [[2 * z, 2 * z + 1] for z in range(chips)]
    both = lax.all_gather(theirs, "mp", axis=0, axis_index_groups=cores)
    pieces = list(call(add_kernel, [((share, width), BF16)] * half, [me_ref], mine, both))
    pieces = pieces[:1] + [
        lax.ppermute(pieces[hop], "mp", [(k, (k + 4 * hop) % heads) for k in range(heads)])
        for hop in range(1, half)
    ]
    (d_user,) = call(
        user_grad_kernel, [((share, width), F32)], [], own_cols, own_out, own_targets, *pieces
    )
    (d_samples,) = call(sample_grad_kernel, [((slots, width), F32)], [], item_recv, own_raw)
    return (loss.reshape(-1), d_user, d_samples)


def solution(mesh):
    placed = (
        P("dp", None),
        P(None, "mp", None),
        P("mp", None, None),
        P("dp", None),
        P("dp", None),
        P(("dp", "mp"), None),
        P(("dp", "mp")),
        P(("dp", "mp")),
    )
    return jax.shard_map(
        per_device,
        mesh=mesh,
        in_specs=placed,
        out_specs=(P("dp"), P(("dp", "mp"), None), P(("dp", "mp"), None)),
        check_vma=False,
    )
```

```python
import functools
import math

import jax
import jax.numpy as jnp
from jax import lax
from jax.experimental import pallas as pl
from jax.experimental.pallas import tpu as pltpu
from jax.sharding import PartitionSpec as P

MAXLEN = 256
INV_TEMP = 20.0
EPSILON = 1e-06
F32 = jnp.float32
BF16 = jnp.bfloat16
STAT_ROWS = 8
FIRST_LIMIT = 62 * 1024 * 1024
VMEM_LIMIT = 40 * 1024 * 1024


def dot(a, b, dims=((1,), (0,))):
    return lax.dot_general(a, b, (dims, ((), ())), preferred_element_type=F32)


def silu(x):
    return x / (1.0 + jnp.exp(-x))


def split3(x):
    hi = x.astype(BF16).astype(F32)
    mid = (x - hi).astype(BF16).astype(F32)
    return hi, mid, x - hi - mid


def unit_rows(values):
    inv_norm = lax.rsqrt(jnp.mean(values * values, -1, keepdims=True) + EPSILON) / math.sqrt(
        values.shape[-1]
    )
    return (values * inv_norm, inv_norm)


def to_columns(rows):
    n = rows[0].shape[1]
    at = lax.broadcasted_iota(jnp.int32, (128, n), 0)
    block = jnp.broadcast_to(rows[-1], (128, n))
    for k in range(len(rows) - 1):
        block = jnp.where(at == k, rows[k], block)
    return block.T


def first_kernel(
    copies, ids_hbm, counts_hbm, lengths_hbm, table_hbm, events_hbm, weight_hbm, out_hbm,
    blocks, own_raw, small, attended_out, gate_out,
    ids, counts, lengths, table, events, weight, out_proj, sem,
):
    slots = own_raw.shape[0]
    count, width = table.shape
    n = events.shape[0]
    dh = out_proj.shape[0]
    loads = []
    for k, (source, target) in enumerate(
        [
            (ids_hbm, ids),
            (counts_hbm, counts),
            (lengths_hbm, lengths),
            (table_hbm, table),
            (events_hbm, events),
            (weight_hbm, weight),
            (out_hbm, out_proj),
        ]
    ):
        loads.append(pltpu.make_async_copy(source, target, sem.at[k]))
        loads[-1].start()

    loads[0].wait()
    loads[1].wait()
    slot = lax.broadcasted_iota(jnp.int32, (slots, count), 0)
    at = lax.broadcasted_iota(jnp.int32, (slots, count), 1)
    wanted = jnp.zeros((slots, count), jnp.int32)
    drawn = jnp.ones((slots, 128), jnp.int32)
    slot_narrow = lax.broadcasted_iota(jnp.int32, (slots, 128), 0)
    for k in range(slots):
        wanted = jnp.where(slot == k, lax.rem(ids[k], count), wanted)
        drawn = jnp.where(slot_narrow == k, counts[k], drawn)
    logs = jnp.log(drawn.astype(F32))
    loads[3].wait()
    raw = dot((at == wanted).astype(F32).astype(BF16), table[...])
    own_raw[...] = raw
    unit, _ = unit_rows(raw)
    pack = jnp.concatenate([unit, logs], 1)
    twice = jnp.concatenate([pack, pack], 0).astype(BF16)
    for k in range(copies // 2):
        blocks[2 * k * slots : 2 * (k + 1) * slots, :] = twice

    loads[2].wait()
    position = lax.broadcasted_iota(jnp.int32, (1, n), 1)
    first = jnp.zeros((1, n), jnp.int32)
    end = jnp.int32(0)
    for k in range(lengths.shape[1]):
        end = end + lengths[0, k]
        first = jnp.where(position >= end, end, first)
    j_at = lax.broadcasted_iota(jnp.int32, (n, n), 0)
    seen = (j_at <= position) & (j_at >= first)
    loads[4].wait()
    wide = events[...].astype(F32)
    normed = (wide * lax.rsqrt(jnp.mean(wide * wide, -1, keepdims=True) + EPSILON)).astype(BF16)
    loads[5].wait()
    proj = silu(dot(normed, weight[...]))
    turned = proj.T
    gate = turned[:dh]
    value = turned[dh : 2 * dh].astype(BF16)
    query = turned[2 * dh : 3 * dh].astype(BF16)
    key = proj[:, 3 * dh :].astype(BF16)
    scores = dot(key, query)
    weights = (jnp.where(seen, silu(scores), 0.0) / MAXLEN).astype(BF16)
    attended = dot(value, weights)
    sums = split3(jnp.sum(attended, 0, keepdims=True))
    squares = split3(jnp.sum(attended * attended, 0, keepdims=True))
    at = lax.broadcasted_iota(jnp.int32, (STAT_ROWS, n), 0)
    loads[6].wait()
    last = out_proj[...].astype(F32)[dh - 1 :]
    rows = jnp.zeros((STAT_ROWS, n), F32)
    for k, row in enumerate(sums + squares + (last,)):
        rows = jnp.where(at == k, row, rows)
    rows = rows.astype(BF16)
    for k in range(small.shape[0]):
        small[k] = rows
    attended_out[...] = attended
    gate_out[...] = gate


def mix_kernel(small, attended, gate, out_proj, payload):
    heads = small.shape[0]
    dh = attended.shape[0]
    stats = small[0].astype(F32)
    for h in range(1, heads):
        stats = stats + small[h].astype(F32)
    full = heads * dh
    row_mean = (stats[0:1] + stats[1:2] + stats[2:3]) / full
    row_sq = (stats[3:4] + stats[4:5] + stats[5:6]) / full
    scale = lax.rsqrt(jnp.maximum(row_sq - row_mean * row_mean, 0.0) + EPSILON)
    payload[0:dh, :] = ((attended[...] - row_mean) * scale * gate[...]).astype(BF16)
    payload[dh:, :] = out_proj[0 : dh - 1, :]


def user_kernel(
    share, me, gathered, small, events, targets,
    positive_row, user_bf, own_out, own_targets, out_rows,
):
    n, width = events.shape
    heads = gathered.shape[0]
    dh = (gathered.shape[1] + 1) // 2
    mixed_in = jnp.concatenate([gathered[h, :dh, :] for h in range(heads)], 0)
    matrix = []
    for h in range(heads):
        matrix += [gathered[h, dh:, :].astype(F32), small[h].astype(F32)[6:7]]
    matrix = jnp.concatenate(matrix, 0).astype(BF16)
    output = events[...].astype(F32) + dot(mixed_in, matrix, ((0,), (0,)))
    out_rows[...] = output
    own = pl.ds(pl.multiple_of(me[0] * share, share), share)
    own_out[...] = out_rows[own, :]
    own_targets[...] = targets[own, :]
    unit, _ = unit_rows(output)
    rounded = unit.astype(BF16)
    user_bf[...] = rounded
    target_unit, _ = unit_rows(targets[...].astype(F32))
    positive = INV_TEMP * jnp.sum(rounded.astype(F32) * target_unit, -1, keepdims=True)
    positive_row[...] = jnp.broadcast_to(positive, (n, 128)).T[0:8]


def neighbours(chips):
    pairs = []
    for k in range(2 * chips):
        z, core = k // 2, k % 2
        step = 1 if z % 2 == core else -1
        pairs.append((k, 2 * ((z + step) % chips) + core))
    return pairs


def score_kernel(me, samples, user_bf, exps, sums, keep, give, chunks):
    width = user_bf.shape[1]
    sample_bf = samples[:, :width]
    log_counts = samples[:, width : width + 128].astype(F32)[:, 0:1]
    neg_exp = jnp.exp(INV_TEMP * dot(sample_bf, user_bf[...], ((1,), (1,))) - log_counts)
    exps[...] = neg_exp
    user_part = dot(neg_exp.astype(BF16), sample_bf, ((0,), (0,))).astype(BF16)
    sums[...] = jnp.broadcast_to(jnp.sum(neg_exp, 0, keepdims=True)[None], sums.shape)
    chips, rows = chunks.shape[:2]
    for z in range(chips):
        chunks[z] = user_part[z * rows : (z + 1) * rows]
    chip, core = me[0] // 2, lax.rem(me[0], 2)
    step = jnp.where(lax.rem(chip, 2) == core, 1, chips - 1)
    for hop in range(chips // 2):
        keep[hop] = chunks[lax.rem(chip + 2 * hop, chips)]
        give[hop] = chunks[lax.rem(chip + step + 2 * hop, chips)]


def grad_kernel(
    share, me, sums, positive_row, exps, user_bf, keep, got,
    loss, item_part, own_cols, mine, theirs, all_cols,
):
    slots = item_part.shape[1]
    positive = positive_row[0:1]
    pos_exp = jnp.exp(positive)
    total = pos_exp
    for k in range(sums.shape[0]):
        total = total + sums[k]
    loss[...] = jnp.log(total) - positive
    probs = (exps[...] / total).astype(BF16)
    part = dot(probs, user_bf[...]).astype(BF16)
    for k in range(item_part.shape[0]):
        item_part[k] = part[k * slots : (k + 1) * slots]
    all_cols[...] = to_columns([1.0 / total, pos_exp / total - 1.0])
    own_cols[...] = all_cols[pl.ds(pl.multiple_of(me[0] * share, share), share), :]
    first_core = lax.rem(me[0], 2) == 0
    for hop in range(keep.shape[0]):
        both = (keep[hop].astype(F32) + got[hop].astype(F32)).astype(BF16)
        mine[hop] = jnp.where(first_core, both[:share], both[share:])
        theirs[hop] = jnp.where(first_core, both[share:], both[:share])


def add_kernel(me, own, both, pieces):
    other = 1 - lax.rem(me[0], 2)
    for hop in range(pieces.shape[0]):
        pieces[hop] = (own[hop].astype(F32) + both[other, hop].astype(F32)).astype(BF16)


def final_kernel(
    me, item_recv, own_raw, own_cols, own_out, own_targets, user_parts, d_user, d_samples
):
    slots = own_raw.shape[0]
    item_sum = item_recv[0].astype(F32)
    for k in range(1, item_recv.shape[0]):
        item_sum = item_sum + item_recv[k].astype(F32)
    own_unit, own_inv = unit_rows(own_raw[...])
    item_grad = INV_TEMP * item_sum
    d_samples[...] = own_inv * (
        item_grad - own_unit * jnp.sum(own_unit * item_grad, -1, keepdims=True)
    )
    user_unit, user_inv = unit_rows(own_out[...])
    target_unit, _ = unit_rows(own_targets[...].astype(F32))
    sources = user_parts.shape[0]
    place = me[0] // 4
    user_part = user_parts[0, lax.rem(place, sources)].astype(F32)
    for k in range(1, sources):
        user_part = user_part + user_parts[k, lax.rem(place + sources - k, sources)].astype(F32)
    user_grad = INV_TEMP * (user_part * own_cols[:, 0:1] + own_cols[:, 1:2] * target_unit)
    d_user[...] = user_inv * (
        user_grad - user_unit * jnp.sum(user_unit * user_grad, -1, keepdims=True)
    )


def call(kernel, outs, scalars, *args, remote=(), scratch=(), limit=VMEM_LIMIT):
    smem = pl.BlockSpec(memory_space=pltpu.SMEM)
    vmem = pl.BlockSpec(memory_space=pltpu.VMEM)
    anywhere = pl.BlockSpec(memory_space=pl.ANY)
    return pl.pallas_call(
        kernel,
        out_shape=[jax.ShapeDtypeStruct(s, t) for s, t in outs],
        in_specs=[smem] * len(scalars) + [anywhere] * len(remote) + [vmem] * len(args),
        out_specs=[vmem] * len(outs),
        scratch_shapes=list(scratch),
        compiler_params=pltpu.CompilerParams(vmem_limit_bytes=limit),
    )(*scalars, *remote, *args)


def per_device(events, in_proj, out_proj, lengths, targets, item_table, sample_ids, sample_counts):
    n, width = events.shape
    dh = out_proj.shape[1]
    heads = lax.axis_size("mp")
    groups = lax.axis_size("dp")
    slots = sample_ids.shape[0]
    scored = slots * groups
    share = n // heads
    me = lax.axis_index("mp")
    me_ref = me.astype(jnp.int32).reshape(1)

    out_rows = out_proj.reshape(dh, width)
    blocks, own_raw, small, attended, gate = call(
        functools.partial(first_kernel, groups),
        [
            ((scored, width + 128), BF16),
            ((slots, width), F32),
            ((heads, STAT_ROWS, n), BF16),
            ((dh, n), F32),
            ((dh, n), F32),
        ],
        [],
        remote=[
            sample_ids,
            sample_counts,
            lengths,
            item_table,
            events,
            in_proj.reshape(width, -1),
            out_rows,
        ],
        scratch=[
            pltpu.SMEM(sample_ids.shape, jnp.int32),
            pltpu.SMEM(sample_counts.shape, jnp.int32),
            pltpu.SMEM(lengths.shape, jnp.int32),
            pltpu.VMEM(item_table.shape, BF16),
            pltpu.VMEM((n, width), BF16),
            pltpu.VMEM((width, 4 * dh), BF16),
            pltpu.VMEM((dh, width), BF16),
            pltpu.SemaphoreType.DMA((7,)),
        ],
        limit=FIRST_LIMIT,
    )
    small = lax.all_to_all(small, "mp", 0, 0, tiled=True)
    small, blocks = lax.optimization_barrier((small, blocks))
    samples = lax.all_to_all(blocks, "dp", 0, 0, tiled=True)
    (payload,) = call(
        mix_kernel, [((2 * dh - 1, n), BF16)], [], small, attended, gate, out_rows
    )
    gathered = lax.all_gather(payload, "mp", axis=0)

    chips = heads // 2
    half = chips // 2
    positive_row, user_bf, own_out, own_targets = call(
        functools.partial(user_kernel, share),
        [((8, n), F32), ((n, width), BF16), ((share, width), F32), ((share, width), BF16)],
        [me_ref],
        gathered,
        small,
        events,
        targets,
        scratch=[pltpu.VMEM((n, width), F32)],
    )
    exps, sums, keep, give = call(
        score_kernel,
        [((scored, n), F32), ((heads, 1, n), F32)] + [((half, 2 * share, width), BF16)] * 2,
        [me_ref],
        samples,
        user_bf,
        scratch=[pltpu.VMEM((chips, 2 * share, width), BF16)],
    )
    got = lax.ppermute(give, "mp", neighbours(chips))
    sums = lax.all_to_all(sums, "mp", 0, 0, tiled=True)
    sums, got = lax.optimization_barrier((sums, got))
    loss, item_part, own_cols, mine, theirs = call(
        functools.partial(grad_kernel, share),
        [((1, n), F32), ((groups, slots, width), BF16), ((share, 128), F32)]
        + [((half, share, width), BF16)] * 2,
        [me_ref],
        sums,
        positive_row,
        exps,
        user_bf,
        keep,
        got,
        scratch=[pltpu.VMEM((n, 128), F32)],
    )
    item_recv = lax.all_to_all(item_part, "dp", 0, 0, tiled=True)
    cores = [[2 * z, 2 * z + 1] for z in range(chips)]
    both = lax.all_gather(theirs, "mp", axis=0, axis_index_groups=cores)
    (pieces,) = call(add_kernel, [((half, share, width), BF16)], [me_ref], mine, both)
    alternate = [[2 * z + c for z in range(p, chips, 2)] for p in range(2) for c in range(2)]
    pieces = lax.all_gather(pieces, "mp", axis=0, axis_index_groups=alternate)
    d_user, d_samples = call(
        final_kernel,
        [((share, width), F32), ((slots, width), F32)],
        [me_ref],
        item_recv,
        own_raw,
        own_cols,
        own_out,
        own_targets,
        pieces,
    )
    return (loss.reshape(-1), d_user, d_samples)


def solution(mesh):
    placed = (
        P("dp", None),
        P(None, "mp", None),
        P("mp", None, None),
        P("dp", None),
        P("dp", None),
        P(("dp", "mp"), None),
        P(("dp", "mp")),
        P(("dp", "mp")),
    )
    return jax.shard_map(
        per_device,
        mesh=mesh,
        in_specs=placed,
        out_specs=(P("dp"), P(("dp", "mp"), None), P(("dp", "mp"), None)),
        check_vma=False,
    )
```

```python
import functools
import math

import jax
import jax.numpy as jnp
from jax import lax
from jax.experimental import pallas as pl
from jax.experimental.pallas import tpu as pltpu
from jax.sharding import PartitionSpec as P

MAXLEN = 256
INV_TEMP = 20.0
EPSILON = 1e-06
F32 = jnp.float32
BF16 = jnp.bfloat16
STAT_ROWS = 8
FIRST_LIMIT = 62 * 1024 * 1024
VMEM_LIMIT = 40 * 1024 * 1024


def dot(a, b, dims=((1,), (0,))):
    return lax.dot_general(a, b, (dims, ((), ())), preferred_element_type=F32)


def silu(x):
    return x / (1.0 + jnp.exp(-x))


def split3(x):
    hi = x.astype(BF16).astype(F32)
    mid = (x - hi).astype(BF16).astype(F32)
    return hi, mid, x - hi - mid


def unit_rows(values):
    inv_norm = lax.rsqrt(jnp.mean(values * values, -1, keepdims=True) + EPSILON) / math.sqrt(
        values.shape[-1]
    )
    return (values * inv_norm, inv_norm)


def to_columns(rows):
    n = rows[0].shape[1]
    at = lax.broadcasted_iota(jnp.int32, (128, n), 0)
    block = jnp.broadcast_to(rows[-1], (128, n))
    for k in range(len(rows) - 1):
        block = jnp.where(at == k, rows[k], block)
    return block.T


def first_kernel(
    copies, ids_hbm, counts_hbm, lengths_hbm, table_hbm, events_hbm, weight_hbm, out_hbm,
    blocks, own_raw, small, attended_out, gate_out,
    ids, counts, lengths, table, events, weight, out_proj, sem,
):
    slots = own_raw.shape[0]
    count, width = table.shape
    n = events.shape[0]
    dh = out_proj.shape[0]
    loads = []
    for k, (source, target) in enumerate(
        [
            (ids_hbm, ids),
            (counts_hbm, counts),
            (lengths_hbm, lengths),
            (table_hbm, table),
            (events_hbm, events),
            (weight_hbm, weight),
            (out_hbm, out_proj),
        ]
    ):
        loads.append(pltpu.make_async_copy(source, target, sem.at[k]))
        loads[-1].start()

    loads[0].wait()
    loads[1].wait()
    slot = lax.broadcasted_iota(jnp.int32, (slots, count), 0)
    at = lax.broadcasted_iota(jnp.int32, (slots, count), 1)
    wanted = jnp.zeros((slots, count), jnp.int32)
    drawn = jnp.ones((slots, 128), jnp.int32)
    slot_narrow = lax.broadcasted_iota(jnp.int32, (slots, 128), 0)
    for k in range(slots):
        wanted = jnp.where(slot == k, lax.rem(ids[k], count), wanted)
        drawn = jnp.where(slot_narrow == k, counts[k], drawn)
    logs = jnp.log(drawn.astype(F32))
    loads[3].wait()
    raw = dot((at == wanted).astype(F32).astype(BF16), table[...])
    own_raw[...] = raw
    unit, _ = unit_rows(raw)
    pack = jnp.concatenate([unit, logs], 1)
    twice = jnp.concatenate([pack, pack], 0).astype(BF16)
    for k in range(copies // 2):
        blocks[2 * k * slots : 2 * (k + 1) * slots, :] = twice

    loads[2].wait()
    position = lax.broadcasted_iota(jnp.int32, (1, n), 1)
    first = jnp.zeros((1, n), jnp.int32)
    end = jnp.int32(0)
    for k in range(lengths.shape[1]):
        end = end + lengths[0, k]
        first = jnp.where(position >= end, end, first)
    j_at = lax.broadcasted_iota(jnp.int32, (n, n), 0)
    seen = (j_at <= position) & (j_at >= first)
    loads[4].wait()
    wide = events[...].astype(F32)
    normed = (wide * lax.rsqrt(jnp.mean(wide * wide, -1, keepdims=True) + EPSILON)).astype(BF16)
    loads[5].wait()
    proj = silu(dot(normed, weight[...]))
    turned = proj.T
    gate = turned[:dh]
    value = turned[dh : 2 * dh].astype(BF16)
    query = turned[2 * dh : 3 * dh].astype(BF16)
    key = proj[:, 3 * dh :].astype(BF16)
    scores = dot(key, query)
    weights = (jnp.where(seen, silu(scores), 0.0) / MAXLEN).astype(BF16)
    attended = dot(value, weights)
    sums = split3(jnp.sum(attended, 0, keepdims=True))
    squares = split3(jnp.sum(attended * attended, 0, keepdims=True))
    at = lax.broadcasted_iota(jnp.int32, (STAT_ROWS, n), 0)
    loads[6].wait()
    last = out_proj[...].astype(F32)[dh - 1 :]
    rows = jnp.zeros((STAT_ROWS, n), F32)
    for k, row in enumerate(sums + squares + (last,)):
        rows = jnp.where(at == k, row, rows)
    rows = rows.astype(BF16)
    for k in range(small.shape[0]):
        small[k] = rows
    attended_out[...] = attended
    gate_out[...] = gate


def mix_kernel(small, attended, gate, out_proj, payload):
    heads = small.shape[0]
    dh = attended.shape[0]
    stats = small[0].astype(F32)
    for h in range(1, heads):
        stats = stats + small[h].astype(F32)
    full = heads * dh
    row_mean = (stats[0:1] + stats[1:2] + stats[2:3]) / full
    row_sq = (stats[3:4] + stats[4:5] + stats[5:6]) / full
    scale = lax.rsqrt(jnp.maximum(row_sq - row_mean * row_mean, 0.0) + EPSILON)
    payload[0:dh, :] = ((attended[...] - row_mean) * scale * gate[...]).astype(BF16)
    payload[dh:, :] = out_proj[0 : dh - 1, :]


def score_kernel(
    share, me, gathered, small, events, targets, samples,
    exps, sums, positive_row, user_bf, keep, give, own_out, own_targets, out_rows, chunks,
):
    n, width = events.shape
    heads = gathered.shape[0]
    dh = (gathered.shape[1] + 1) // 2
    mixed_in = jnp.concatenate([gathered[h, :dh, :] for h in range(heads)], 0)
    matrix = []
    for h in range(heads):
        matrix += [gathered[h, dh:, :].astype(F32), small[h].astype(F32)[6:7]]
    matrix = jnp.concatenate(matrix, 0).astype(BF16)
    mixed = dot(mixed_in, matrix, ((0,), (0,)))
    output = events[...].astype(F32) + mixed
    out_rows[...] = output
    own = pl.ds(pl.multiple_of(me[0] * share, share), share)
    own_out[...] = out_rows[own, :]
    own_targets[...] = targets[own, :]
    unit, _ = unit_rows(output)
    rounded = unit.astype(BF16)
    user_bf[...] = rounded
    target_unit, _ = unit_rows(targets[...].astype(F32))
    positive = INV_TEMP * jnp.sum(rounded.astype(F32) * target_unit, -1, keepdims=True)
    positive_row[...] = jnp.broadcast_to(positive, (n, 128)).T[0:8]
    sample_bf = samples[:, :width]
    log_counts = samples[:, width : width + 128].astype(F32)[:, 0:1]
    neg_exp = jnp.exp(INV_TEMP * dot(sample_bf, rounded, ((1,), (1,))) - log_counts)
    exps[...] = neg_exp
    user_part = dot(neg_exp.astype(BF16), sample_bf, ((0,), (0,))).astype(BF16)
    sums[...] = jnp.broadcast_to(jnp.sum(neg_exp, 0, keepdims=True)[None], sums.shape)
    chips, rows = chunks.shape[:2]
    half = chips // 2
    for z in range(chips):
        chunks[z] = user_part[z * rows : (z + 1) * rows]
    chip = me[0] // 2
    neighbour = chip + 1 - 2 * lax.rem(chip, 2)
    for hop in range(half):
        keep[hop] = chunks[lax.rem(chip + 2 * hop, chips)]
        give[hop] = chunks[lax.rem(neighbour + 2 * hop, chips)]


def grad_kernel(
    share, me, sums, positive_row, exps, user_bf, keep, got,
    loss, item_part, own_cols, mine, theirs, all_cols,
):
    slots = item_part.shape[1]
    positive = positive_row[0:1]
    pos_exp = jnp.exp(positive)
    total = pos_exp
    for k in range(sums.shape[0]):
        total = total + sums[k]
    loss[...] = jnp.log(total) - positive
    probs = (exps[...] / total).astype(BF16)
    part = dot(probs, user_bf[...]).astype(BF16)
    for k in range(item_part.shape[0]):
        item_part[k] = part[k * slots : (k + 1) * slots]
    all_cols[...] = to_columns([1.0 / total, pos_exp / total - 1.0])
    own_cols[...] = all_cols[pl.ds(pl.multiple_of(me[0] * share, share), share), :]
    first_core = lax.rem(me[0], 2) == 0
    for hop in range(keep.shape[0]):
        both = (keep[hop].astype(F32) + got[hop].astype(F32)).astype(BF16)
        mine[hop] = jnp.where(first_core, both[:share], both[share:])
        theirs[hop] = jnp.where(first_core, both[share:], both[:share])


def add_kernel(me, own, both, *pieces):
    other = 1 - lax.rem(me[0], 2)
    for hop in range(len(pieces)):
        pieces[hop][...] = (own[hop].astype(F32) + both[other, hop].astype(F32)).astype(BF16)


def final_kernel(item_recv, own_raw, own_cols, own_out, own_targets, *refs):
    user_parts, (d_user, d_samples) = refs[:-2], refs[-2:]
    slots = own_raw.shape[0]
    item_sum = item_recv[0].astype(F32)
    for k in range(1, item_recv.shape[0]):
        item_sum = item_sum + item_recv[k].astype(F32)
    own_unit, own_inv = unit_rows(own_raw[...])
    item_grad = INV_TEMP * item_sum
    d_samples[...] = own_inv * (
        item_grad - own_unit * jnp.sum(own_unit * item_grad, -1, keepdims=True)
    )
    user_unit, user_inv = unit_rows(own_out[...])
    target_unit, _ = unit_rows(own_targets[...].astype(F32))
    user_part = user_parts[0][...].astype(F32)
    for part in user_parts[1:]:
        user_part = user_part + part[...].astype(F32)
    user_grad = INV_TEMP * (user_part * own_cols[:, 0:1] + own_cols[:, 1:2] * target_unit)
    d_user[...] = user_inv * (
        user_grad - user_unit * jnp.sum(user_unit * user_grad, -1, keepdims=True)
    )


def call(kernel, outs, scalars, *args, remote=(), scratch=(), limit=VMEM_LIMIT):
    smem = pl.BlockSpec(memory_space=pltpu.SMEM)
    vmem = pl.BlockSpec(memory_space=pltpu.VMEM)
    anywhere = pl.BlockSpec(memory_space=pl.ANY)
    return pl.pallas_call(
        kernel,
        out_shape=[jax.ShapeDtypeStruct(s, t) for s, t in outs],
        in_specs=[smem] * len(scalars) + [anywhere] * len(remote) + [vmem] * len(args),
        out_specs=[vmem] * len(outs),
        scratch_shapes=list(scratch),
        compiler_params=pltpu.CompilerParams(vmem_limit_bytes=limit),
    )(*scalars, *remote, *args)


def per_device(events, in_proj, out_proj, lengths, targets, item_table, sample_ids, sample_counts):
    n, width = events.shape
    dh = out_proj.shape[1]
    heads = lax.axis_size("mp")
    groups = lax.axis_size("dp")
    slots = sample_ids.shape[0]
    scored = slots * groups
    share = n // heads
    me = lax.axis_index("mp")
    me_ref = me.astype(jnp.int32).reshape(1)

    out_rows = out_proj.reshape(dh, width)
    blocks, own_raw, small, attended, gate = call(
        functools.partial(first_kernel, groups),
        [
            ((scored, width + 128), BF16),
            ((slots, width), F32),
            ((heads, STAT_ROWS, n), BF16),
            ((dh, n), F32),
            ((dh, n), F32),
        ],
        [],
        remote=[
            sample_ids,
            sample_counts,
            lengths,
            item_table,
            events,
            in_proj.reshape(width, -1),
            out_rows,
        ],
        scratch=[
            pltpu.SMEM(sample_ids.shape, jnp.int32),
            pltpu.SMEM(sample_counts.shape, jnp.int32),
            pltpu.SMEM(lengths.shape, jnp.int32),
            pltpu.VMEM(item_table.shape, BF16),
            pltpu.VMEM((n, width), BF16),
            pltpu.VMEM((width, 4 * dh), BF16),
            pltpu.VMEM((dh, width), BF16),
            pltpu.SemaphoreType.DMA((7,)),
        ],
        limit=FIRST_LIMIT,
    )
    small = lax.all_to_all(small, "mp", 0, 0, tiled=True)
    small, blocks = lax.optimization_barrier((small, blocks))
    samples = lax.all_to_all(blocks, "dp", 0, 0, tiled=True)
    (payload,) = call(
        mix_kernel, [((2 * dh - 1, n), BF16)], [], small, attended, gate, out_rows
    )
    gathered = lax.all_gather(payload, "mp", axis=0)

    chips = heads // 2
    half = chips // 2
    exps, sums, positive_row, user_bf, keep, give, own_out, own_targets = call(
        functools.partial(score_kernel, share),
        [
            ((scored, n), F32),
            ((heads, 1, n), F32),
            ((8, n), F32),
            ((n, width), BF16),
            ((half, 2 * share, width), BF16),
            ((half, 2 * share, width), BF16),
            ((share, width), F32),
            ((share, width), BF16),
        ],
        [me_ref],
        gathered,
        small,
        events,
        targets,
        samples,
        scratch=[pltpu.VMEM((n, width), F32), pltpu.VMEM((chips, 2 * share, width), BF16)],
    )
    got = lax.ppermute(give, "mp", [(k, k ^ 2) for k in range(heads)])
    sums = lax.all_to_all(sums, "mp", 0, 0, tiled=True)
    sums, got = lax.optimization_barrier((sums, got))
    loss, item_part, own_cols, mine, theirs = call(
        functools.partial(grad_kernel, share),
        [((1, n), F32), ((groups, slots, width), BF16), ((share, 128), F32)]
        + [((half, share, width), BF16)] * 2,
        [me_ref],
        sums,
        positive_row,
        exps,
        user_bf,
        keep,
        got,
        scratch=[pltpu.VMEM((n, 128), F32)],
    )
    item_recv = lax.all_to_all(item_part, "dp", 0, 0, tiled=True)
    cores = [[2 * z, 2 * z + 1] for z in range(chips)]
    both = lax.all_gather(theirs, "mp", axis=0, axis_index_groups=cores)
    pieces = list(call(add_kernel, [((share, width), BF16)] * half, [me_ref], mine, both))
    pieces = pieces[:1] + [
        lax.ppermute(pieces[hop], "mp", [(k, (k + 4 * hop) % heads) for k in range(heads)])
        for hop in range(1, half)
    ]
    d_user, d_samples = call(
        final_kernel,
        [((share, width), F32), ((slots, width), F32)],
        [],
        item_recv,
        own_raw,
        own_cols,
        own_out,
        own_targets,
        *pieces,
    )
    return (loss.reshape(-1), d_user, d_samples)


def solution(mesh):
    placed = (
        P("dp", None),
        P(None, "mp", None),
        P("mp", None, None),
        P("dp", None),
        P("dp", None),
        P(("dp", "mp"), None),
        P(("dp", "mp")),
        P(("dp", "mp")),
    )
    return jax.shard_map(
        per_device,
        mesh=mesh,
        in_specs=placed,
        out_specs=(P("dp"), P(("dp", "mp"), None), P(("dp", "mp"), None)),
        check_vma=False,
    )
```
